32 devices in a mesh: tok: 8 (over z, y), voc: 4 (over x, core).
Axes of the slice: x: 2, y: 2, z: 4, core: 2. Of those that a mesh axis runs over, the one named last changes fastest.
Arguments:
- hidden: bfloat16 [2048, 1536], P('tok'), may hold values from -1000 to 1000
- norm_gain: float32 [1536], replicated, may hold values from 0.1 to 1.9
- head_weight: bfloat16 [1536, 49152], P(None, ('tok', 'voc')), may hold values from -8 to 8
- targets: int32 [2048], P('tok'), may hold values from 0 to 49151
- lengths: int32 [8], replicated, may hold values from 1 to 256, 1280 in all
- prior_device: int32 [8], replicated, may hold values from 0 to 7, each once
- prior_row: int32 [8], replicated, may hold values from 0 to 255
Outputs:
- logprob: float32 [2048], P('tok')
- entropy: float32 [2048], P('tok')
The draws below stay inside these ranges and needn't reach their ends.
Inputs may be any that keep to these rules, and one draw needn't show every extreme that they name: One turn's block is full, lengths[t] = 256. `prior_device`: every block index appears once.
All inputs are finite; a program needn't handle non-finite values.
Results may differ from the reference program's by a relative error of at most 0.0036.
Values may be sent and summed in bfloat16 or wider, within the bound.
No kernel may reach another device: no remote copies, remote signals or barrier semaphores. Data moves between devices by JAX's collectives and lax.ppermute only.
A program may use at most 192 MiB of HBM per device.

```python
import math
import jax
import jax.numpy as jnp
import numpy as np
from jax import lax

D = 1536
V = 49152
TOK_DEV = 256
TURNS = 8
TOKENS = 2048
LIVE_TOTAL = 1280


def drawn_dirs(key):
    return jnp.sign(jax.random.normal(jax.random.fold_in(key, 77), (8, 4, D), jnp.float32) + 0.001)


def draw_head_weight(key, part):
    noise = jnp.clip(jax.random.normal(jax.random.fold_in(key, 1), (D, V), jnp.float32), -5.0, 5.0)
    feature_scale = jnp.exp(jax.random.uniform(jax.random.fold_in(key, 8), (D, 1), jnp.float32) * math.log(4.0)) / 2.326
    spread = jnp.exp(jax.random.uniform(jax.random.fold_in(key, 2), (1, V), jnp.float32) * math.log(1.2))
    ramp = 0.9 + 0.2 * jnp.arange(V, dtype=jnp.float32)[None, :] / V
    weight = noise * feature_scale * spread * ramp * (3.8 / math.sqrt(D))
    direct = drawn_dirs(key).reshape(32, D).T
    strength = np.tile(1.0 + 0.5 * np.arange(4), 8)
    columns = np.array([j * (V // 8) + 2 * m for j in range(8) for m in range(4)])
    leading = direct * jnp.asarray(123.0 * strength / D, jnp.float32)[None, :]
    partner = leading * jnp.asarray(1.0 - 2.0 / (123.0 * strength), jnp.float32)[None, :]
    weight = weight.at[:, columns].set(leading).at[:, columns + 1].set(partner)
    return weight.astype(jnp.bfloat16)


def draw_hidden(key, part):
    noise = jnp.clip(jax.random.normal(jax.random.fold_in(key, 3), (TOKENS, D), jnp.float32), -5.0, 5.0)
    row_scale = jnp.exp(jax.random.uniform(jax.random.fold_in(key, 4), (TOKENS, 1), jnp.float32) * math.log(10.0))
    col_scale = jnp.exp(jax.random.uniform(jax.random.fold_in(key, 5), (1, D), jnp.float32) * math.log(10.0))
    values = noise * row_scale * col_scale
    turn_count = TOKENS // TOK_DEV
    rows = np.array([t * TOK_DEV + m for t in range(turn_count) for m in range(4)])
    first_ids = np.array([t % 8 for t in range(turn_count) for m in range(4)])
    second_ids = np.array([m for t in range(turn_count) for m in range(4)])
    direct = drawn_dirs(key)[first_ids, second_ids]
    values = values.at[rows].set(direct)
    return values.astype(jnp.bfloat16)


def plant(values, key, low, high):
    spot = [jax.random.randint(jax.random.fold_in(key, axis), (), 0, length) for axis, length in enumerate(values.shape)]
    main_axis = values.shape.index(max(values.shape))
    neighbour = spot[:main_axis] + [(spot[main_axis] + 1) % values.shape[main_axis]] + spot[main_axis + 1:]
    return values.at[tuple(spot)].set(low).at[tuple(neighbour)].set(high)


def rank_bounds(count, slope):
    loads = [(1 << 20) // math.isqrt(grade ** slope) + 1 for grade in range(1, count + 1)]
    scale = 1 + sum(loads) // (1 << 30)
    return np.cumsum(np.array([max(1, weight // scale) for weight in loads]))


def ranked(key, extent, number_of, lean):
    grid = rank_bounds(number_of, lean)
    lot = jax.random.randint(jax.random.fold_in(key, 1), extent, 0, int(grid[number_of - 1]))
    standing = jnp.searchsorted(jnp.asarray(grid, jnp.int32), lot, side="right")
    return jax.random.permutation(jax.random.fold_in(key, 2), number_of)[standing].astype(jnp.int32)


def length_profile(amount, total, limit, skew):
    weights = [(1 << 20) // math.isqrt(grade ** skew) + 1 for grade in range(2, amount + 1)]
    rest, given = total - limit - (amount - 1), [1] * (amount - 1)
    while rest > 0:
        candidates = [i for i in range(amount - 1) if given[i] < limit]
        whole, remaining = sum([weights[i] for i in candidates]), rest
        for i in candidates:
            addition = min(limit - given[i], max(1, remaining * weights[i] // whole), rest)
            given[i] = given[i] + addition
            rest = rest - addition
    return np.array([limit] + given)


def ragged(stream_key, number_of, total, most, lean):
    if number_of == 2:
        one = jax.random.randint(stream_key, (), max(1, total - most), min(most, total - 1) + 1)
        return jnp.stack([one, total - one])
    sizes = jnp.asarray(length_profile(number_of, total, most, lean), jnp.int32)
    twos = (number_of - 1) // 2
    source_of, taker = sizes[1:1 + 2 * twos:2], sizes[2:2 + 2 * twos:2]
    slack = jnp.minimum(source_of - 1, most - taker)
    shifted = jax.random.randint(jax.random.fold_in(stream_key, 1), (twos,), 0, 1 << 20) % (slack + 1)
    sizes = sizes.at[1:1 + 2 * twos:2].set(source_of - shifted).at[2:2 + 2 * twos:2].set(taker + shifted)
    return sizes[jax.random.permutation(jax.random.fold_in(stream_key, 2), number_of)]


def setup_inputs(seed: int = 0) -> dict:
    key_of = jax.random.split(jax.random.key(seed), 8)
    hidden = draw_hidden(jax.random.fold_in(key_of[7], 71), 0)
    norm_gain = jnp.clip(1.0 + 0.18 * jax.random.normal(key_of[1], (D,), jnp.float32), 0.1, 1.9)
    head_weight = draw_head_weight(jax.random.fold_in(key_of[7], 71), 0)
    targets = plant(ranked(key_of[3], (TOKENS,), V, 2), jax.random.fold_in(key_of[3], 3), 0, V - 1).astype(jnp.int32)
    lengths = ragged(key_of[4], TURNS, LIVE_TOTAL, TOK_DEV, 2).astype(jnp.int32)
    prior_device = jax.random.permutation(key_of[5], TURNS).astype(jnp.int32)
    prior_row = plant(jax.random.randint(key_of[6], (TURNS,), 0, TOK_DEV), jax.random.fold_in(key_of[6], 1), 0, TOK_DEV - 1).astype(jnp.int32)
    return dict(hidden=hidden, norm_gain=norm_gain, head_weight=head_weight, targets=targets, lengths=lengths, prior_device=prior_device, prior_row=prior_row)


epsilon = 1e-05

def reference(hidden, norm_gain, head_weight, targets, lengths, prior_device, prior_row):
    blocks = hidden.reshape(TURNS, TOK_DEV, D)
    prior = blocks[prior_device, prior_row]
    scored = jnp.concatenate([prior[:, None, :], blocks[:, :-1, :]], axis=1).astype(jnp.float32)
    normed = (scored * lax.rsqrt(lax.optimization_barrier(jnp.mean(scored * scored, axis=2, keepdims=True)) + epsilon) * norm_gain.astype(jnp.float32)).astype(jnp.bfloat16)
    target_rows = targets.reshape(TURNS, TOK_DEV)

    def score(inputs):
        states, wanted = inputs
        logits = jnp.dot(states, head_weight, preferred_element_type=jnp.float32)
        largest = lax.optimization_barrier(jnp.max(logits, axis=1))
        weights = jnp.exp(logits - largest[:, None])
        totals = lax.optimization_barrier(jnp.sum(weights, axis=1))
        moments = lax.optimization_barrier(jnp.sum(weights * logits, axis=1))
        picked = jnp.take_along_axis(logits, wanted[:, None], axis=1)[:, 0]
        normalizer = largest + jnp.log(totals)
        return (picked - normalizer, normalizer - moments / totals)
    logprob, entropy = lax.map(score, (normed, target_rows))
    valid = jnp.arange(TOK_DEV, dtype=jnp.int32)[None, :] < lengths[:, None]
    logprob = jnp.where(valid, logprob, 0.0).reshape(TOKENS)
    entropy = jnp.where(valid, entropy, 0.0).reshape(TOKENS)
    return (logprob, entropy)
```

```python
import functools

import jax
import jax.numpy as jnp
from jax import lax
from jax.experimental import pallas as pl
from jax.experimental.pallas import tpu as pltpu
from jax.sharding import PartitionSpec as P

epsilon = 1e-05
LANES = 128
SUB = 16
AXES = ("tok", "voc")


def score_kernel(layout, rows, width, nblocks, table, first, turns, targets, gain, head, *rest):
    pieces = rest[: len(layout)]
    out, states, logits, part_max, part_sum, part_moment, part_pick = rest[len(layout) :]
    feats = states.shape[1]
    tiles = head.shape[1] // LANES
    scale = gain[...]

    slot = 0
    for ref, count in zip(pieces, layout):
        size = ref.shape[0] // count
        for piece in range(count):
            place = table[slot]
            slot += 1

            def norm_rows(step, _, ref=ref, piece=piece, size=size, place=place):
                at = pl.multiple_of(piece * size + step * SUB, SUB)
                to = pl.multiple_of(place + step * SUB, SUB)
                value = ref[pl.ds(at, SUB), :].astype(jnp.float32)
                mean = jnp.sum(value * value, axis=1, keepdims=True) * (1.0 / feats)
                states[pl.ds(to, SUB), :] = (value * lax.rsqrt(mean + epsilon) * scale).astype(jnp.bfloat16)
                return 0

            lax.fori_loop(0, size // SUB, norm_rows, 0, unroll=2)

    me, base = table[slot], table[slot + 1]
    total_rows = nblocks * rows
    logits[...] = jnp.dot(states[...], head[...], preferred_element_type=jnp.float32)

    lane = lax.broadcasted_iota(jnp.int32, (1, rows), 1)
    for block in range(nblocks):
        position = table[slot + 2] + block
        turn = me ^ position
        prior_target = jnp.int32(0)
        for u in range(turns.shape[0]):
            prior_target = jnp.where(turns[u] == turn, first[u ^ me], prior_target)
        own = targets[pl.ds(position, 1), :]
        shifted = jnp.concatenate([own[:, 1:], own[:, :1]], axis=1)
        wanted = jnp.where(lane == rows - 1, prior_target, shifted) - base
        column = jnp.broadcast_to(wanted.astype(jnp.float32), (LANES, rows)).T
        part_pick[pl.ds(block * rows, rows), :] = column

    lanes = lax.broadcasted_iota(jnp.int32, (SUB, LANES), 1)
    lanes_f = lanes.astype(jnp.float32)

    def stats_rows(step, _):
        at = pl.ds(pl.multiple_of(step * SUB, SUB), SUB)

        def tile_of(k):
            value = logits[at, k * LANES : (k + 1) * LANES]
            if (k + 1) * LANES > width:
                value = jnp.where(lanes < width - k * LANES, value, -1e30)
            return value

        top = tile_of(0)
        for k in range(1, tiles):
            top = jnp.maximum(top, tile_of(k))
        offset = part_pick[at, :] - lanes_f
        total = jnp.zeros((SUB, LANES), jnp.float32)
        moment = total
        picked = total
        for k in range(tiles):
            value = tile_of(k)
            weight = jnp.exp(value - top)
            total = total + weight
            moment = moment + weight * value
            picked = picked + jnp.where(offset == float(k * LANES), value, 0.0)
        part_max[at, :] = top
        part_sum[at, :] = total
        part_moment[at, :] = moment
        part_pick[at, :] = picked
        return 0

    lax.fori_loop(0, total_rows // SUB, stats_rows, 0, unroll=2)

    halves = rows // LANES
    for block in range(nblocks):
        for half in range(halves):
            at = pl.ds(block * rows + half * LANES, LANES)
            top = part_max[at, :].T
            largest = jnp.max(top, axis=0, keepdims=True)
            factor = jnp.exp(top - largest)
            out[block, half : half + 1, :] = largest
            out[block, halves + half : halves + half + 1, :] = jnp.sum(part_sum[at, :].T * factor, axis=0, keepdims=True)
            out[block, 2 * halves + half : 2 * halves + half + 1, :] = jnp.sum(
                part_moment[at, :].T * factor, axis=0, keepdims=True
            )
            out[block, 3 * halves + half : 3 * halves + half + 1, :] = jnp.sum(part_pick[at, :].T, axis=0, keepdims=True)


def score(pieces, layout, table, first, turns, targets, gain, head, rows, width, nblocks):
    total_rows = nblocks * rows
    feats = gain.shape[1]
    columns = head.shape[1]
    smem = pl.BlockSpec(memory_space=pltpu.SMEM)
    vmem = pl.BlockSpec(memory_space=pltpu.VMEM)
    return pl.pallas_call(
        functools.partial(score_kernel, layout, rows, width, nblocks),
        out_shape=jax.ShapeDtypeStruct((nblocks, 4 * (rows // LANES), LANES), jnp.float32),
        in_specs=[smem] * 3 + [vmem] * (3 + len(pieces)),
        out_specs=vmem,
        scratch_shapes=[
            pltpu.VMEM((total_rows, feats), jnp.bfloat16),
            pltpu.VMEM((total_rows, columns), jnp.float32),
        ]
        + [pltpu.VMEM((total_rows, LANES), jnp.float32)] * 4,
        compiler_params=pltpu.CompilerParams(vmem_limit_bytes=40 * 1024 * 1024),
        cost_estimate=pl.CostEstimate(
            flops=2 * total_rows * feats * columns,
            bytes_accessed=2 * feats * (total_rows + columns),
            transcendentals=total_rows * columns,
        ),
    )(table, first, turns, targets, gain, head, *pieces)


def collect_kernel(turn_count, voc_count, tail, table, turns, *rest):
    stats, out, held = rest[:-2], rest[-2], rest[-1]
    me = table[0]
    per = stats[0].shape[0]
    for index, ref in enumerate(stats):
        for block in range(per):
            held[(index * per + block) ^ me] = ref[block]
    shape = held.shape[1:]
    row = lax.broadcasted_iota(jnp.int32, shape, 0)
    lane = lax.broadcasted_iota(jnp.int32, shape, 1)
    swap = (lane == LANES - 1) & (row % tail == tail - 1)
    for turn in range(turn_count):
        value = jnp.where(swap, held[turns[turn]], held[turn])
        for copy in range(voc_count):
            out[turn * voc_count + copy] = value


def collect(stats, table, turns, turn_count, voc_count):
    smem = pl.BlockSpec(memory_space=pltpu.SMEM)
    vmem = pl.BlockSpec(memory_space=pltpu.VMEM)
    sublanes = stats[0].shape[1]
    return pl.pallas_call(
        functools.partial(collect_kernel, turn_count, voc_count, sublanes // 4),
        out_shape=jax.ShapeDtypeStruct((turn_count * voc_count, sublanes, LANES), jnp.float32),
        in_specs=[smem] * 2 + [vmem] * len(stats),
        out_specs=vmem,
        scratch_shapes=[pltpu.VMEM((turn_count, sublanes, LANES), jnp.float32)],
    )(table, turns, *stats)


def finish_kernel(table, lengths, received, logprob, entropy):
    halves = received.shape[1] // 4
    top = received[:, 0:halves, :]
    largest = jnp.max(top, axis=0)
    factor = jnp.exp(top - largest[None])
    total = jnp.sum(received[:, halves : 2 * halves, :] * factor, axis=0)
    moment = jnp.sum(received[:, 2 * halves : 3 * halves, :] * factor, axis=0)
    picked = jnp.sum(received[:, 3 * halves :, :], axis=0)
    normalizer = largest + jnp.log(total)
    half = lax.broadcasted_iota(jnp.int32, largest.shape, 0)
    lane = lax.broadcasted_iota(jnp.int32, largest.shape, 1)
    live = half * LANES + lane < lengths[table[0]]

    def by_scored_row(value):
        previous = jnp.concatenate([value[halves - 1 :], value[: halves - 1]], axis=0)
        rolled = jnp.concatenate([value[:, LANES - 1 :], value[:, : LANES - 1]], axis=1)
        rolled_previous = jnp.concatenate([previous[:, LANES - 1 :], previous[:, : LANES - 1]], axis=1)
        return jnp.where(live, jnp.where(lane == 0, rolled_previous, rolled), 0.0)

    logprob[...] = by_scored_row(picked - normalizer)
    entropy[...] = by_scored_row(normalizer - moment / total)


def finish(table, lengths, received):
    smem = pl.BlockSpec(memory_space=pltpu.SMEM)
    vmem = pl.BlockSpec(memory_space=pltpu.VMEM)
    halves = received.shape[1] // 4
    shape = jax.ShapeDtypeStruct((halves, LANES), jnp.float32)
    return pl.pallas_call(
        finish_kernel, out_shape=(shape, shape), in_specs=[smem, smem, vmem], out_specs=(vmem, vmem)
    )(table, lengths, received)


def after(value, *others):
    return lax.optimization_barrier((value,) + others)[0]


def body(hidden, norm_gain, head_weight, targets, lengths, prior_device, prior_row):
    rows, feats = hidden.shape
    width = head_weight.shape[1]
    tok_count, voc_count = lax.axis_size("tok"), lax.axis_size("voc")
    side = voc_count // 2
    depth = tok_count // side
    me, band = lax.axis_index("tok"), lax.axis_index("voc")
    core = band % 2
    quarter = rows // voc_count
    half = rows // 2

    def permute(value, move):
        pairs = []
        for t in range(tok_count):
            for v in range(voc_count):
                to_t, to_v = move(t, v)
                pairs.append((t * voc_count + v, to_t * voc_count + to_v))
        return lax.ppermute(value, AXES, pairs)

    def along_z(value, d):
        return permute(value, lambda t, v: (t ^ (d * side), v))

    def along_y(value, d):
        return permute(value, lambda t, v: (t ^ d, v))

    def across_cores(value):
        return permute(value, lambda t, v: (t, v ^ 1))

    def second_hop(value, d):
        return permute(value, lambda t, v: (t ^ d, v) if v % 2 == 0 else (t, v ^ (2 * d)))

    def third_hop(value, d):
        return permute(value, lambda t, v: (t, v ^ (2 * d)) if v % 2 == 0 else (t ^ d, v))

    asked = jnp.sum(jnp.where(prior_device == me, prior_row, 0))
    asked_state = lax.dynamic_slice_in_dim(hidden, asked, 1, 0)
    row_ids = lax.broadcasted_iota(jnp.int32, (rows, 1), 0)
    block = jnp.where(row_ids == rows - 1, asked_state, hidden)

    own_quarter = lax.dynamic_slice_in_dim(block, band * quarter, quarter, 0)
    own_half = lax.dynamic_slice_in_dim(block, core * half, half, 0)

    near = [along_y(own_half, d) for d in range(1, side)]
    arrived = {1: along_z(own_quarter, 1)}
    for d in range(2, depth):
        arrived[d] = along_z(own_quarter if d == 2 else after(own_quarter, arrived[d - 2]), d)

    known = targets.reshape(1, rows)
    step = 1
    while step < tok_count:
        moved = lax.ppermute(known, "tok", [(i, i ^ step) for i in range(tok_count)])
        known = jnp.concatenate([known, moved], axis=0)
        step *= 2
    first = known[:, 0]
    base = (me * voc_count + band) * width
    gain = norm_gain.reshape(1, feats)
    head = head_weight
    if width % LANES:
        head = jnp.pad(head_weight, ((0, 0), (0, LANES - width % LANES)))

    def places(core_id, band_id):
        result = []
        for d in range(side):
            y, x = jnp.where(core_id == 0, d, 0), jnp.where(core_id == 0, 0, d)
            result.append(y * rows + (band_id ^ (2 * x)) * quarter)
        for d in range(1, side):
            for e in range(side):
                y, x = jnp.where(core_id == 0, e, d), jnp.where(core_id == 0, d, e)
                result.append(y * rows + (band_id ^ (2 * x)) * quarter)
        return result

    common = [me, base]
    stats = []
    pieces = [block]
    where = [0]
    layout = [1]
    for d in range(1, side):
        pieces += [near[d - 1], across_cores(near[d - 1])]
        where += [d * rows + core * half, d * rows + (1 - core) * half]
        layout += [1, 1]
    table = jnp.stack([jnp.asarray(p, jnp.int32) for p in where + common + [0]])
    stats.append(score(pieces, layout, table, first, prior_device, known, gain, head, rows, width, side))

    where = places(core, band) + places(1 - core, band ^ 1)
    for d in range(1, depth):
        near_pieces = [arrived[d]] + [second_hop(arrived[d], e) for e in range(1, side)]
        gathered = jnp.concatenate(near_pieces, axis=0)
        far = [third_hop(gathered, e) for e in range(1, side)]
        pieces = [gathered] + far + [across_cores(gathered)] + [across_cores(f) for f in far]
        table = jnp.stack([jnp.asarray(p, jnp.int32) for p in where + common + [d * side]])
        stats.append(
            score(pieces, [side] * len(pieces), table, first, prior_device, known, gain, head, rows, width, side)
        )

    spot = jnp.reshape(me, (1,)).astype(jnp.int32)
    sent = collect(stats, spot, prior_device, tok_count, voc_count)
    received = lax.all_to_all(sent, AXES, 0, 0)
    logprob, entropy = finish(spot, lengths, received)
    return logprob.reshape(rows), entropy.reshape(rows)


def solution(mesh):
    in_specs = (P("tok", None), P(), P(None, ("tok", "voc")), P("tok"), P(), P(), P())
    out_specs = (P("tok"), P("tok"))
    return jax.shard_map(body, mesh=mesh, in_specs=in_specs, out_specs=out_specs, check_vma=False)
```

```python
import functools

import jax
import jax.numpy as jnp
from jax import lax
from jax.experimental import pallas as pl
from jax.experimental.pallas import tpu as pltpu
from jax.sharding import PartitionSpec as P

epsilon = 1e-05
LANES = 128
SUB = 16
GROUP = 32
DIGIT = 256
AXES = ("tok", "voc")
VMEM_LIMIT = 24 * 1024 * 1024


def prepare_kernel(spot, *refs):
    sources, (block, quarter, half, table), held, arrivals = refs[:6], refs[6:10], refs[10:16], refs[16]
    fetches = [pltpu.make_async_copy(sources[i], held[i], arrivals.at[i]) for i in range(6)]
    for fetch in fetches:
        fetch.start()
    for fetch in fetches:
        fetch.wait()
    hidden, gain, targets, lengths, turns, prior_rows = held
    rows, feats = hidden.shape
    me, band = spot[0], spot[1]
    scale = gain[...].reshape(1, feats)
    table[0] = me
    table[1] = band
    for u in range(turns.shape[0]):
        table[2 + u] = turns[u]
        table[2 + turns.shape[0] + u] = lengths[u]

    own = targets[...].reshape(1, rows).astype(jnp.float32)
    own = jnp.concatenate([own[:, 1:], own[:, :1]], axis=1)
    high = jnp.floor(own * (1.0 / DIGIT))
    low = own - high * DIGIT
    lane = lax.broadcasted_iota(jnp.int32, (LANES, LANES), 1)
    first_high = jnp.broadcast_to(high[:, rows - 1 :], (LANES, LANES))
    first_low = jnp.broadcast_to(low[:, rows - 1 :], (LANES, LANES))
    for start in range(0, rows, LANES):
        at = slice(start, start + LANES)
        own_high = jnp.broadcast_to(high[:, at], (LANES, LANES)).T
        own_low = jnp.broadcast_to(low[:, at], (LANES, LANES)).T
        digits = jnp.where(
            lane < LANES // 2,
            jnp.where(lane < LANES // 4, own_high, own_low),
            jnp.where(lane < 3 * LANES // 4, first_high, first_low),
        )
        block[at, feats:] = digits.astype(jnp.bfloat16)

    def norm_rows(step, _):
        at = pl.ds(pl.multiple_of(step * SUB, SUB), SUB)
        value = hidden[at, :].astype(jnp.float32)
        mean = jnp.sum(value * value, axis=1, keepdims=True) * (1.0 / feats)
        block[at, 0:feats] = (value * lax.rsqrt(mean + epsilon) * scale).astype(jnp.bfloat16)
        return 0

    lax.fori_loop(0, rows // SUB, norm_rows, 0, unroll=4)
    asked = jnp.int32(0)
    for u in range(turns.shape[0]):
        asked = jnp.where(turns[u] == me, prior_rows[u], asked)
    end = lengths[me] - 1
    sub = lax.broadcasted_iota(jnp.int32, (SUB, 1), 0)
    values = block[pl.ds(pl.multiple_of(asked // SUB * SUB, SUB), SUB), 0:feats].astype(jnp.float32)
    value = jnp.sum(jnp.where(sub == asked % SUB, values, 0.0), axis=0, keepdims=True)
    at = pl.ds(pl.multiple_of(end // SUB * SUB, SUB), SUB)
    present = block[at, 0:feats].astype(jnp.float32)
    block[at, 0:feats] = jnp.where(sub == end % SUB, value, present).astype(jnp.bfloat16)
    quarter[...] = block[pl.ds(pl.multiple_of(band * quarter.shape[0], SUB), quarter.shape[0]), :]
    half[...] = block[pl.ds(pl.multiple_of(band % 2 * half.shape[0], SUB), half.shape[0]), :]


def prepare(spot, hidden, gain, targets, lengths, turns, prior_rows, voc_count):
    rows, feats = hidden.shape
    sources = (hidden, gain, targets, lengths, turns, prior_rows)
    sources = [pltpu.with_memory_space_constraint(a, pltpu.HBM) for a in sources]
    smem, vmem = pl.BlockSpec(memory_space=pltpu.SMEM), pl.BlockSpec(memory_space=pltpu.VMEM)
    shapes = [jax.ShapeDtypeStruct((n, feats + LANES), hidden.dtype) for n in (rows, rows // voc_count, rows // 2)]
    shapes.append(jax.ShapeDtypeStruct((2 + 2 * turns.shape[0],), jnp.int32))
    held = [pltpu.VMEM(a.shape, a.dtype) for a in sources[:3]] + [pltpu.SMEM(a.shape, a.dtype) for a in sources[3:]]
    return pl.pallas_call(
        prepare_kernel,
        out_shape=shapes,
        in_specs=[smem] + [pl.BlockSpec(memory_space=pltpu.HBM)] * 6,
        out_specs=[vmem] * 3 + [smem],
        scratch_shapes=held + [pltpu.SemaphoreType.DMA((6,))],
        compiler_params=pltpu.CompilerParams(vmem_limit_bytes=VMEM_LIMIT),
    )(spot, *sources)


def place_of(kind, core, band, rows, side, voc_count):
    name, d, e = kind
    if name == "own":
        return 0
    if name == "near":
        return d * rows + (core if e == 0 else 1 - core) * (rows // 2)
    if name == "other":
        core, band = 1 - core, band ^ 1
    y, x = jnp.where(core == 0, e, d), jnp.where(core == 0, d, e)
    return y * rows + (band ^ (2 * x)) * (rows // voc_count)


def score_kernel(
    layout, position, rows, width, nblocks, turn_count, voc_count, spans, collects, loads, table, head, *rest
):
    pieces, rest = rest[: len(layout)], rest[len(layout) :]
    earlier, rest = rest[: 2 * len(spans)], rest[2 * len(spans) :]
    out, rest = rest[0], rest[1:]
    if not collects:
        ends, rest = rest[0], rest[1:]
    if loads:
        stored, head, arrival, rest = head, rest[0], rest[1], rest[2:]
        fetch = pltpu.make_async_copy(stored, head, arrival)
        fetch.start()
    if collects:
        held, rest = rest[0], rest[1:]
    states, even, odd, lines, kept, edges = rest
    feats = head.shape[0]
    tiles = head.shape[1] // LANES
    halves = rows // LANES
    side = voc_count // 2
    turns, lengths = 2, 2 + turn_count
    me, band = table[0], table[1]
    core = band % 2
    base = (me * voc_count + band) * width

    offsets = []
    live = []
    offset = jnp.int32(0)
    for block in range(nblocks):
        length = table[lengths + (me ^ (position + block))]
        offsets.append(offset)
        live.append(length)
        offset = offset + (length + GROUP - 1) // GROUP * GROUP
    total_rows = offset + GROUP if collects else offset
    count = (total_rows + LANES - 1) // LANES

    for ref, parts in zip(pieces, layout):
        size = ref.shape[0] // len(parts)
        for index, (kind, start_block) in enumerate(parts):
            place = place_of(kind, core, band, rows, side, voc_count)
            block = start_block + place // rows
            row = place % rows
            to, length = offsets[0], live[0]
            for b in range(1, nblocks):
                to = jnp.where(block == b, offsets[b], to)
                length = jnp.where(block == b, live[b], length)
            for step in range(0, size, GROUP):

                @pl.when(row + step < length)
                def _(ref=ref, start=index * size + step, to=to + row + step):
                    states[pl.ds(pl.multiple_of(to, GROUP), GROUP), :] = ref[start : start + GROUP, :]

    sub = lax.broadcasted_iota(jnp.int32, (SUB, 1), 0)
    sub_group = lax.broadcasted_iota(jnp.int32, (GROUP, 1), 0)
    edge = jnp.zeros(edges.shape, jnp.float32)
    for ref in earlier[1::2]:
        edge = edge + ref[...].astype(jnp.float32)
    edges[...] = edge
    for block in range(nblocks):
        end = offsets[block] + live[block] - 1
        values = states[pl.ds(pl.multiple_of(end // SUB * SUB, SUB), SUB), 0:feats].astype(jnp.float32)
        line = position + block
        edges[line : line + 1, 0:feats] = jnp.sum(jnp.where(sub == end % SUB, values, 0.0), axis=0, keepdims=True)
        values = states[pl.ds(pl.multiple_of(offsets[block], SUB), SUB), feats:].astype(jnp.float32)
        edges[line : line + 1, feats:] = values[0:1, :]
    if collects:
        group = pl.ds(pl.multiple_of(offset, GROUP), GROUP)
        states[group, 0:feats] = edges[:, 0:feats].astype(jnp.bfloat16)
        digits = jnp.zeros((GROUP, LANES), jnp.float32)
        for line in range(turn_count):
            asked = me ^ table[turns + (me ^ line)]
            digits = digits + jnp.where(sub_group == asked, edges[line : line + 1, feats:], 0.0)
        states[group, feats:] = pltpu.roll(digits, LANES // 2, 1).astype(jnp.bfloat16)
    else:
        ends[...] = edges[...].astype(jnp.bfloat16)

    lanes = lax.broadcasted_iota(jnp.int32, (SUB, LANES), 1)
    lanes_f = lanes.astype(jnp.float32)
    base_f = base.astype(jnp.float32)

    def multiply(tile, into):
        at = pl.ds(pl.multiple_of(tile * LANES, LANES), LANES)
        into[...] = jnp.dot(states[at, 0:feats], head[...], preferred_element_type=jnp.float32)

    def reduce(tile, logits):
        for row in range(0, LANES, SUB):
            at = slice(row, row + SUB)

            def part(k, at=at):
                value = logits[at, k * LANES : (k + 1) * LANES]
                if (k + 1) * LANES > width:
                    value = jnp.where(lanes < width - k * LANES, value, -1e30)
                return value

            top = part(0)
            for k in range(1, tiles):
                top = jnp.maximum(top, part(k))
            here = pl.ds(pl.multiple_of(tile * LANES + row, SUB), SUB)
            digits = states[here, feats:].astype(jnp.float32)
            digits = jnp.where(lanes < LANES // 4, digits * DIGIT, jnp.where(lanes < LANES // 2, digits, 0.0))
            digits = digits + pltpu.roll(digits, LANES // 2, 1)
            offset = digits + pltpu.roll(digits, LANES // 4, 1) - base_f - lanes_f
            total = jnp.zeros((SUB, LANES), jnp.float32)
            moment = total
            picked = total
            for k in range(tiles):
                value = part(k)
                weight = jnp.exp(value - top)
                total = total + weight
                moment = moment + weight * value
                picked = picked + jnp.where(offset == float(k * LANES), value, 0.0)
            kept[0, at, :] = top
            kept[1, at, :] = total
            kept[2, at, :] = moment
            kept[3, at, :] = picked
        top = kept[0].T
        largest = jnp.max(top, axis=0, keepdims=True)
        factor = jnp.exp(top - largest)
        lines[tile, 0:1, :] = largest
        lines[tile, 1:2, :] = jnp.sum(kept[1].T * factor, axis=0, keepdims=True)
        lines[tile, 2:3, :] = jnp.sum(kept[2].T * factor, axis=0, keepdims=True)
        lines[tile, 3:4, :] = jnp.sum(kept[3].T, axis=0, keepdims=True)

    if loads:
        fetch.wait()
    multiply(0, even)

    def two_tiles(step, _):
        multiply(2 * step + 1, odd)
        reduce(2 * step, even)
        multiply(2 * step + 2, even)
        reduce(2 * step + 1, odd)
        return 0

    lax.fori_loop(0, (count - 1) // 2, two_tiles, 0)

    @pl.when(count % 2 == 0)
    def _():
        multiply(count - 1, odd)
        reduce(count - 2, even)
        reduce(count - 1, odd)

    @pl.when(count % 2 == 1)
    def _():
        reduce(count - 1, even)

    def line_of(block_offset, half):
        tile, turned = block_offset // LANES + half, block_offset % LANES
        back = (LANES - turned) % LANES
        here, next_one = pltpu.roll(lines[tile], back, 1), pltpu.roll(lines[tile + 1], back, 1)
        return jnp.where(lax.broadcasted_iota(jnp.int32, here.shape, 1) < LANES - turned, here, next_one)

    high = 4 * halves
    for block in range(nblocks):
        to = held.at[me ^ (position + block)] if collects else out.at[block]
        for half in range(halves):
            to[4 * half : 4 * half + 4, :] = line_of(offsets[block], half)[0:4, :]

    if collects:
        for start, ref in zip(spans, earlier[0::2]):
            for block in range(ref.shape[0]):
                held[me ^ (start + block)] = ref[block]
        line = lax.broadcasted_iota(jnp.int32, (high, LANES), 0)
        lane = lax.broadcasted_iota(jnp.int32, (high, LANES), 1)
        swap = (lane == LANES - 1) & (line >= high - 4)
        edge_lines = jnp.concatenate([lines[offset // LANES, 0:4, :]] * halves, axis=0)
        for turn in range(turn_count):
            at = offset % LANES + (me ^ table[turns + turn])
            prior = pltpu.roll(edge_lines, LANES - 1 - at, 1)
            value = jnp.where(swap, prior, held[turn])
            for copy in range(voc_count):
                out[turn * voc_count + copy] = value


def score(pieces, layout, table, position, head, rows, width, nblocks, turn_count, voc_count, earlier=(), spans=(), loads=False):
    collects = bool(spans) or nblocks == turn_count
    total_rows = nblocks * rows + LANES
    feats, columns = head.shape
    high = 4 * (rows // LANES)
    smem = pl.BlockSpec(memory_space=pltpu.SMEM)
    vmem = pl.BlockSpec(memory_space=pltpu.VMEM)
    where_head = vmem
    blocks = turn_count * voc_count if collects else nblocks
    result = [jax.ShapeDtypeStruct((blocks, high, LANES), jnp.float32)]
    scratch = []
    if not collects:
        result.append(jax.ShapeDtypeStruct((GROUP, feats + LANES), jnp.bfloat16))
    if loads:
        head = pltpu.with_memory_space_constraint(head, pltpu.HBM)
        where_head = pl.BlockSpec(memory_space=pltpu.HBM)
        result.append(pltpu.VMEM((feats, columns), head.dtype))
        scratch.append(pltpu.SemaphoreType.DMA)
    if collects:
        scratch.append(pltpu.VMEM((turn_count, high, LANES), jnp.float32))
    return pl.pallas_call(
        functools.partial(
            score_kernel, layout, position, rows, width, nblocks, turn_count, voc_count, spans, collects, loads
        ),
        out_shape=result,
        in_specs=[smem, where_head] + [vmem] * (len(pieces) + len(earlier)),
        out_specs=[vmem] * len(result),
        scratch_shapes=scratch
        + [
            pltpu.VMEM((total_rows, feats + LANES), jnp.bfloat16),
            pltpu.VMEM((LANES, columns), jnp.float32),
            pltpu.VMEM((LANES, columns), jnp.float32),
            pltpu.VMEM((total_rows // LANES + 1, 8, LANES), jnp.float32),
            pltpu.VMEM((4, LANES, LANES), jnp.float32),
            pltpu.VMEM((GROUP, feats + LANES), jnp.float32),
        ],
        compiler_params=pltpu.CompilerParams(vmem_limit_bytes=VMEM_LIMIT),
        cost_estimate=pl.CostEstimate(
            flops=2 * total_rows * feats * columns,
            bytes_accessed=2 * feats * (total_rows + columns),
            transcendentals=total_rows * columns,
        ),
    )(table, head, *pieces, *earlier)


def finish_kernel(spot, lengths, received, logprob, entropy):
    halves = received.shape[1] // 4

    def kind_of(kind):
        return jnp.concatenate([received[:, 4 * h + kind : 4 * h + kind + 1, :] for h in range(halves)], axis=1)

    top = kind_of(0)
    largest = jnp.max(top, axis=0)
    factor = jnp.exp(top - largest[None])
    total = jnp.sum(kind_of(1) * factor, axis=0)
    moment = jnp.sum(kind_of(2) * factor, axis=0)
    picked = jnp.sum(kind_of(3), axis=0)
    normalizer = largest + jnp.log(total)
    half = lax.broadcasted_iota(jnp.int32, largest.shape, 0)
    lane = lax.broadcasted_iota(jnp.int32, largest.shape, 1)
    live = half * LANES + lane < lengths[spot[0]]

    def by_scored_row(value):
        previous = jnp.concatenate([value[halves - 1 :], value[: halves - 1]], axis=0)
        rolled = jnp.concatenate([value[:, LANES - 1 :], value[:, : LANES - 1]], axis=1)
        rolled_previous = jnp.concatenate([previous[:, LANES - 1 :], previous[:, : LANES - 1]], axis=1)
        return jnp.where(live, jnp.where(lane == 0, rolled_previous, rolled), 0.0)

    logprob[...] = by_scored_row(picked - normalizer)
    entropy[...] = by_scored_row(normalizer - moment / total)


def finish(spot, lengths, received):
    smem = pl.BlockSpec(memory_space=pltpu.SMEM)
    vmem = pl.BlockSpec(memory_space=pltpu.VMEM)
    halves = received.shape[1] // 4
    shape = jax.ShapeDtypeStruct((halves, LANES), jnp.float32)
    return pl.pallas_call(
        finish_kernel, out_shape=(shape, shape), in_specs=[smem, smem, vmem], out_specs=(vmem, vmem)
    )(spot, lengths, received)


def after(value, *others):
    return lax.optimization_barrier((value,) + others)[0]


def body(hidden, norm_gain, head_weight, targets, lengths, prior_device, prior_row):
    rows, feats = hidden.shape
    width = head_weight.shape[1]
    tok_count, voc_count = lax.axis_size("tok"), lax.axis_size("voc")
    side = voc_count // 2
    depth = tok_count // side
    me, band = lax.axis_index("tok"), lax.axis_index("voc")
    core = band % 2
    quarter = rows // voc_count
    half = rows // 2

    def permute(value, move):
        pairs = []
        for t in range(tok_count):
            for v in range(voc_count):
                to_t, to_v = move(t, v)
                pairs.append((t * voc_count + v, to_t * voc_count + to_v))
        return lax.ppermute(value, AXES, pairs)

    def along_z(value, d):
        return permute(value, lambda t, v: (t ^ (d * side), v))

    def along_y(value, d):
        return permute(value, lambda t, v: (t ^ d, v))

    def across_cores(value):
        return permute(value, lambda t, v: (t, v ^ 1))

    def second_hop(value, d):
        return permute(value, lambda t, v: (t ^ d, v) if v % 2 == 0 else (t, v ^ (2 * d)))

    def third_hop(value, d):
        return permute(value, lambda t, v: (t, v ^ (2 * d)) if v % 2 == 0 else (t ^ d, v))

    spot = jnp.stack([me, band]).astype(jnp.int32)
    block, own_quarter, own_half, table = prepare(
        spot, hidden, norm_gain, targets, lengths, prior_device, prior_row, voc_count
    )
    near = [along_y(own_half, d) for d in range(1, side)]
    arrived = {1: along_z(own_quarter, 1)}
    for d in range(2, depth):
        high = 1 << (d.bit_length() - 1)
        arrived[d] = along_z(after(arrived[high], arrived[1]) if d > high else own_quarter, d % high or high)
    near_far = [across_cores(n) for n in near]

    head = head_weight
    if width % LANES:
        head = jnp.pad(head_weight, ((0, 0), (0, LANES - width % LANES)))

    pieces, layout = [block], [((("own", 0, 0), 0),)]
    for d in range(1, side):
        pieces += [near[d - 1], near_far[d - 1]]
        layout += [((("near", d, 0), 0),), ((("near", d, 1), 0),)]
    groups = [(pieces, layout)]
    sizes = (rows, width, 2 * side, tok_count, voc_count)
    second, third = {}, {}
    for d in range(1, depth):
        start = after(arrived[d], arrived[1]) if d > 1 else arrived[d]
        second[d] = [second_hop(start, e) for e in range(1, side)]
        gathered = jnp.concatenate([start] + second[d], axis=0)
        if d > 1:
            gathered = after(gathered, *third[1])
        third[d] = [third_hop(gathered, e) for e in range(1, side)]
        far = list(third[d])
        if d == depth - 1:
            joined = [sum(parts, []) for parts in zip(*groups[:2])]
            first_stats, first_ends, head = score(*joined, table, 0, head, *sizes, loads=True)
            far = [after(f, first_stats) for f in far]
        pieces = [gathered, across_cores(gathered)]
        for f in far:
            pieces += [f, across_cores(f)]
        first_block = (d * side) % (2 * side) if d > 1 else side
        layout = []
        for e in range(side):
            for name in ("same", "other"):
                layout.append(tuple(((name, e, i), first_block) for i in range(side)))
        groups.append((pieces, layout))

    joined = [sum(parts, []) for parts in zip(*groups[2:])]
    (sent,) = score(*joined, table, 2 * side, head, *sizes, earlier=(first_stats, first_ends), spans=(0,))
    received = lax.all_to_all(sent, AXES, 0, 0)
    logprob, entropy = finish(spot, lengths, received)
    return logprob.reshape(rows), entropy.reshape(rows)


def solution(mesh):
    in_specs = (P("tok", None), P(), P(None, ("tok", "voc")), P("tok"), P(), P(), P())
    out_specs = (P("tok"), P("tok"))
    return jax.shard_map(body, mesh=mesh, in_specs=in_specs, out_specs=out_specs, check_vma=False)
```

```python
import functools

import jax
import jax.numpy as jnp
from jax import lax
from jax.experimental import pallas as pl
from jax.experimental.pallas import tpu as pltpu
from jax.sharding import PartitionSpec as P

epsilon = 1e-05
LANES = 128
SUB = 16
GROUP = 32
DIGIT = 256
AXES = ("tok", "voc")
VMEM_LIMIT = 24 * 1024 * 1024


def prepare_kernel(spot, *refs):
    sources, (block, quarter, half, table), held, arrivals = refs[:6], refs[6:10], refs[10:16], refs[16]
    fetches = [pltpu.make_async_copy(sources[i], held[i], arrivals.at[i]) for i in range(6)]
    for fetch in fetches:
        fetch.start()
    for fetch in fetches:
        fetch.wait()
    hidden, gain, targets, lengths, turns, prior_rows = held
    rows, feats = hidden.shape
    me, band = spot[0], spot[1]
    scale = gain[...].reshape(1, feats)
    table[0] = me
    table[1] = band
    for u in range(turns.shape[0]):
        table[2 + u] = turns[u]
        table[2 + turns.shape[0] + u] = lengths[u]

    own = targets[...].reshape(1, rows).astype(jnp.float32)
    own = jnp.concatenate([own[:, 1:], own[:, :1]], axis=1)
    high = jnp.floor(own * (1.0 / DIGIT))
    low = own - high * DIGIT
    lane = lax.broadcasted_iota(jnp.int32, (LANES, LANES), 1)
    first_high = jnp.broadcast_to(high[:, rows - 1 :], (LANES, LANES))
    first_low = jnp.broadcast_to(low[:, rows - 1 :], (LANES, LANES))
    for start in range(0, rows, LANES):
        at = slice(start, start + LANES)
        own_high = jnp.broadcast_to(high[:, at], (LANES, LANES)).T
        own_low = jnp.broadcast_to(low[:, at], (LANES, LANES)).T
        digits = jnp.where(
            lane < LANES // 2,
            jnp.where(lane < LANES // 4, own_high, own_low),
            jnp.where(lane < 3 * LANES // 4, first_high, first_low),
        )
        block[at, feats:] = digits.astype(jnp.bfloat16)

    def norm_rows(step, _):
        at = pl.ds(pl.multiple_of(step * SUB, SUB), SUB)
        value = hidden[at, :].astype(jnp.float32)
        mean = jnp.sum(value * value, axis=1, keepdims=True) * (1.0 / feats)
        block[at, 0:feats] = (value * lax.rsqrt(mean + epsilon) * scale).astype(jnp.bfloat16)
        return 0

    lax.fori_loop(0, rows // SUB, norm_rows, 0, unroll=4)
    asked = jnp.int32(0)
    for u in range(turns.shape[0]):
        asked = jnp.where(turns[u] == me, prior_rows[u], asked)
    end = lengths[me] - 1
    sub = lax.broadcasted_iota(jnp.int32, (SUB, 1), 0)
    values = block[pl.ds(pl.multiple_of(asked // SUB * SUB, SUB), SUB), 0:feats].astype(jnp.float32)
    value = jnp.sum(jnp.where(sub == asked % SUB, values, 0.0), axis=0, keepdims=True)
    at = pl.ds(pl.multiple_of(end // SUB * SUB, SUB), SUB)
    present = block[at, 0:feats].astype(jnp.float32)
    block[at, 0:feats] = jnp.where(sub == end % SUB, value, present).astype(jnp.bfloat16)
    quarter[...] = block[pl.ds(pl.multiple_of(band * quarter.shape[0], SUB), quarter.shape[0]), :]
    half[...] = block[pl.ds(pl.multiple_of(band % 2 * half.shape[0], SUB), half.shape[0]), :]


def prepare(spot, hidden, gain, targets, lengths, turns, prior_rows, voc_count):
    rows, feats = hidden.shape
    sources = (hidden, gain, targets, lengths, turns, prior_rows)
    sources = [pltpu.with_memory_space_constraint(a, pltpu.HBM) for a in sources]
    smem, vmem = pl.BlockSpec(memory_space=pltpu.SMEM), pl.BlockSpec(memory_space=pltpu.VMEM)
    shapes = [jax.ShapeDtypeStruct((n, feats + LANES), hidden.dtype) for n in (rows, rows // voc_count, rows // 2)]
    shapes.append(jax.ShapeDtypeStruct((2 + 2 * turns.shape[0],), jnp.int32))
    held = [pltpu.VMEM(a.shape, a.dtype) for a in sources[:3]] + [pltpu.SMEM(a.shape, a.dtype) for a in sources[3:]]
    return pl.pallas_call(
        prepare_kernel,
        out_shape=shapes,
        in_specs=[smem] + [pl.BlockSpec(memory_space=pltpu.HBM)] * 6,
        out_specs=[vmem] * 3 + [smem],
        scratch_shapes=held + [pltpu.SemaphoreType.DMA((6,))],
        compiler_params=pltpu.CompilerParams(vmem_limit_bytes=VMEM_LIMIT),
    )(spot, *sources)


def place_of(kind, core, band, rows, side, voc_count):
    name, d, e, index = kind
    quarter = rows // voc_count
    if name == "own":
        return index * quarter
    if name == "near":
        return d * rows + (core if e == 0 else 1 - core) * (rows // 2) + index * quarter
    if name == "other":
        core, band = 1 - core, band ^ 1
    y, x = jnp.where(core == 0, index, d), jnp.where(core == 0, d, index)
    return y * rows + (band ^ (2 * x)) * quarter


def score_kernel(layout, rows, width, turn_count, voc_count, collects, loads, table, head, *rest):
    pieces, rest = rest[: len(layout)], rest[len(layout) :]
    if collects:
        earlier, earlier_ends, rest = rest[0], rest[1], rest[2:]
        out, rest = rest[0], rest[1:]
    else:
        out, ends, rest = rest[0], rest[1], rest[2:]
    if loads:
        stored, head, arrival, rest = head, rest[0], rest[1], rest[2:]
        fetch = pltpu.make_async_copy(stored, head, arrival)
        fetch.start()
    found = out
    if collects:
        found, rest = rest[0], rest[1:]
    states, even, odd, lines, kept, edges = rest
    feats = head.shape[0]
    tiles = head.shape[1] // LANES
    halves = rows // LANES
    side = voc_count // 2
    size = rows // voc_count
    turns, lengths = 2, 2 + turn_count
    me, band = table[0], table[1]
    core = band % 2
    base = (me * voc_count + band) * width

    offset = jnp.int32(0)
    moved = []
    present = set()
    for ref, parts in zip(pieces, layout):
        for index, (kind, start_block) in enumerate(parts):
            present.update(range(start_block, start_block + side))
            place = jnp.asarray(place_of(kind, core, band, rows, side, voc_count), jnp.int32)
            block = start_block + place // rows
            row = place % rows
            live = jnp.clip(table[lengths + (me ^ block)] - row, 0, size)
            for step in range(0, size, GROUP):

                @pl.when(step < live)
                def _(ref=ref, start=index * size + step, to=offset + step):
                    states[pl.ds(pl.multiple_of(to, GROUP), GROUP), :] = ref[start : start + GROUP, :]

            moved.append((start_block, block, row, offset))
            offset = offset + (live + GROUP - 1) // GROUP * GROUP
    total_rows = offset + GROUP if collects else offset
    count = (total_rows + LANES - 1) // LANES

    sub = lax.broadcasted_iota(jnp.int32, (SUB, 1), 0)
    sub_group = lax.broadcasted_iota(jnp.int32, (GROUP, 1), 0)
    edges[...] = earlier_ends[...].astype(jnp.float32) if collects else jnp.zeros(edges.shape, jnp.float32)
    for line in sorted(present):
        end = table[lengths + (me ^ line)] - 1
        end_row = end // size * size
        at_end, at_first = jnp.int32(-1), jnp.int32(-1)
        for start_block, block, row, to in moved:
            if start_block <= line < start_block + side:
                at_end = jnp.where((block == line) & (row == end_row), to + end % size, at_end)
                at_first = jnp.where((block == line) & (row == 0), to, at_first)

        def row_at(at, columns):
            group = pl.ds(pl.multiple_of(jnp.maximum(at, 0) // SUB * SUB, SUB), SUB)
            values = states[group, columns].astype(jnp.float32)
            return jnp.sum(jnp.where((sub == at % SUB) & (at >= 0), values, 0.0), axis=0, keepdims=True)

        for at, columns in ((at_end, slice(0, feats)), (at_first, slice(feats, feats + LANES))):
            edges[line : line + 1, columns] = edges[line : line + 1, columns] + row_at(at, columns)
    if collects:
        group = pl.ds(pl.multiple_of(offset, GROUP), GROUP)
        states[group, 0:feats] = edges[:, 0:feats].astype(jnp.bfloat16)
        digits = jnp.zeros((GROUP, LANES), jnp.float32)
        for line in range(turn_count):
            asked = me ^ table[turns + (me ^ line)]
            digits = digits + jnp.where(sub_group == asked, edges[line : line + 1, feats:], 0.0)
        states[group, feats:] = pltpu.roll(digits, LANES // 2, 1).astype(jnp.bfloat16)
    else:
        ends[...] = edges[...].astype(jnp.bfloat16)

    lanes = lax.broadcasted_iota(jnp.int32, (SUB, LANES), 1)
    lanes_f = lanes.astype(jnp.float32)
    base_f = base.astype(jnp.float32)

    def multiply(tile, into):
        at = pl.ds(pl.multiple_of(tile * LANES, LANES), LANES)
        into[...] = jnp.dot(states[at, 0:feats], head[...], preferred_element_type=jnp.float32)

    def reduce(tile, logits):
        for row in range(0, LANES, SUB):
            at = slice(row, row + SUB)

            def part(k, at=at):
                value = logits[at, k * LANES : (k + 1) * LANES]
                if (k + 1) * LANES > width:
                    value = jnp.where(lanes < width - k * LANES, value, -1e30)
                return value

            top = part(0)
            for k in range(1, tiles):
                top = jnp.maximum(top, part(k))
            here = pl.ds(pl.multiple_of(tile * LANES + row, SUB), SUB)
            digits = states[here, feats:].astype(jnp.float32)
            digits = jnp.where(lanes < LANES // 4, digits * DIGIT, jnp.where(lanes < LANES // 2, digits, 0.0))
            digits = digits + pltpu.roll(digits, LANES // 2, 1)
            offset = digits + pltpu.roll(digits, LANES // 4, 1) - base_f - lanes_f
            total = jnp.zeros((SUB, LANES), jnp.float32)
            moment = total
            picked = total
            for k in range(tiles):
                value = part(k)
                weight = jnp.exp(value - top)
                total = total + weight
                moment = moment + weight * value
                picked = picked + jnp.where(offset == float(k * LANES), value, 0.0)
            kept[0, at, :] = top
            kept[1, at, :] = total
            kept[2, at, :] = moment
            kept[3, at, :] = picked
        top = kept[0].T
        largest = jnp.max(top, axis=0, keepdims=True)
        factor = jnp.exp(top - largest)
        lines[tile, 0:1, :] = largest
        lines[tile, 1:2, :] = jnp.sum(kept[1].T * factor, axis=0, keepdims=True)
        lines[tile, 2:3, :] = jnp.sum(kept[2].T * factor, axis=0, keepdims=True)
        lines[tile, 3:4, :] = jnp.sum(kept[3].T, axis=0, keepdims=True)

    if loads:
        fetch.wait()
    multiply(0, even)

    def two_tiles(step, _):
        multiply(2 * step + 1, odd)
        reduce(2 * step, even)
        multiply(2 * step + 2, even)
        reduce(2 * step + 1, odd)
        return 0

    lax.fori_loop(0, (count - 1) // 2, two_tiles, 0)

    @pl.when(count % 2 == 0)
    def _():
        multiply(count - 1, odd)
        reduce(count - 2, even)
        reduce(count - 1, odd)

    @pl.when(count % 2 == 1)
    def _():
        reduce(count - 1, even)

    lane = lax.broadcasted_iota(jnp.int32, (8, LANES), 1)
    if collects:
        found[...] = earlier[...]
    for _, block, row, to in moved:
        tile, turned, shift = to // LANES, to % LANES, row % LANES
        back = (LANES - turned) % LANES
        here, following = pltpu.roll(lines[tile], back, 1), pltpu.roll(lines[tile + 1], back, 1)
        value = pltpu.roll(jnp.where(lane < LANES - turned, here, following), shift, 1)
        inside = (lane >= shift) & (lane < shift + size)
        found[block, row // LANES] = jnp.where(inside, value, found[block, row // LANES])

    if collects:
        high = 4 * halves
        line = lax.broadcasted_iota(jnp.int32, (high, LANES), 0)
        lane = lax.broadcasted_iota(jnp.int32, (high, LANES), 1)
        swap = (lane == LANES - 1) & (line >= high - 4)
        edge_lines = jnp.concatenate([lines[offset // LANES, 0:4, :]] * halves, axis=0)
        for turn in range(turn_count):
            at = offset % LANES + (me ^ table[turns + turn])
            prior = pltpu.roll(edge_lines, LANES - 1 - at, 1)
            own = jnp.concatenate([found[me ^ turn, half][0:4, :] for half in range(halves)], axis=0)
            value = jnp.where(swap, prior, own)
            for copy in range(voc_count):
                out[turn * voc_count + copy] = value


def score(pieces, layout, table, head, rows, width, turn_count, voc_count, earlier=(), loads=False):
    collects = bool(earlier)
    raw_rows = sum(piece.shape[0] for piece in pieces)
    feats, columns = head.shape
    halves = rows // LANES
    smem = pl.BlockSpec(memory_space=pltpu.SMEM)
    vmem = pl.BlockSpec(memory_space=pltpu.VMEM)
    where_head = vmem
    by_block = (turn_count, halves, 8, LANES)
    scratch = []
    if collects:
        result = [jax.ShapeDtypeStruct((turn_count * voc_count, 4 * halves, LANES), jnp.float32)]
    else:
        result = [jax.ShapeDtypeStruct(by_block, jnp.float32)]
        result.append(jax.ShapeDtypeStruct((GROUP, feats + LANES), jnp.bfloat16))
    if loads:
        head = pltpu.with_memory_space_constraint(head, pltpu.HBM)
        where_head = pl.BlockSpec(memory_space=pltpu.HBM)
        result.append(pltpu.VMEM((feats, columns), head.dtype))
        scratch.append(pltpu.SemaphoreType.DMA)
    if collects:
        scratch.append(pltpu.VMEM(by_block, jnp.float32))
    return pl.pallas_call(
        functools.partial(score_kernel, layout, rows, width, turn_count, voc_count, collects, loads),
        out_shape=result,
        in_specs=[smem, where_head] + [vmem] * (len(pieces) + len(earlier)),
        out_specs=[vmem] * len(result),
        scratch_shapes=scratch
        + [
            pltpu.VMEM((raw_rows + LANES, feats + LANES), jnp.bfloat16),
            pltpu.VMEM((LANES, columns), jnp.float32),
            pltpu.VMEM((LANES, columns), jnp.float32),
            pltpu.VMEM((raw_rows // LANES + 2, 8, LANES), jnp.float32),
            pltpu.VMEM((4, LANES, LANES), jnp.float32),
            pltpu.VMEM((GROUP, feats + LANES), jnp.float32),
        ],
        compiler_params=pltpu.CompilerParams(vmem_limit_bytes=VMEM_LIMIT),
        cost_estimate=pl.CostEstimate(
            flops=2 * raw_rows * feats * columns,
            bytes_accessed=2 * feats * (raw_rows + columns),
            transcendentals=raw_rows * columns,
        ),
    )(table, head, *pieces, *earlier)


def finish_kernel(spot, lengths, received, logprob, entropy):
    halves = received.shape[1] // 4

    def kind_of(kind):
        return jnp.concatenate([received[:, 4 * h + kind : 4 * h + kind + 1, :] for h in range(halves)], axis=1)

    top = kind_of(0)
    largest = jnp.max(top, axis=0)
    factor = jnp.exp(top - largest[None])
    total = jnp.sum(kind_of(1) * factor, axis=0)
    moment = jnp.sum(kind_of(2) * factor, axis=0)
    picked = jnp.sum(kind_of(3), axis=0)
    normalizer = largest + jnp.log(total)
    half = lax.broadcasted_iota(jnp.int32, largest.shape, 0)
    lane = lax.broadcasted_iota(jnp.int32, largest.shape, 1)
    live = half * LANES + lane < lengths[spot[0]]

    def by_scored_row(value):
        previous = jnp.concatenate([value[halves - 1 :], value[: halves - 1]], axis=0)
        rolled = jnp.concatenate([value[:, LANES - 1 :], value[:, : LANES - 1]], axis=1)
        rolled_previous = jnp.concatenate([previous[:, LANES - 1 :], previous[:, : LANES - 1]], axis=1)
        return jnp.where(live, jnp.where(lane == 0, rolled_previous, rolled), 0.0)

    logprob[...] = by_scored_row(picked - normalizer)
    entropy[...] = by_scored_row(normalizer - moment / total)


def finish(spot, lengths, received):
    smem = pl.BlockSpec(memory_space=pltpu.SMEM)
    vmem = pl.BlockSpec(memory_space=pltpu.VMEM)
    halves = received.shape[1] // 4
    shape = jax.ShapeDtypeStruct((halves, LANES), jnp.float32)
    return pl.pallas_call(
        finish_kernel, out_shape=(shape, shape), in_specs=[smem, smem, vmem], out_specs=(vmem, vmem)
    )(spot, lengths, received)


def after(value, *others):
    return lax.optimization_barrier((value,) + others)[0]


def body(hidden, norm_gain, head_weight, targets, lengths, prior_device, prior_row):
    rows, feats = hidden.shape
    width = head_weight.shape[1]
    tok_count, voc_count = lax.axis_size("tok"), lax.axis_size("voc")
    side = voc_count // 2
    depth = tok_count // side
    me, band = lax.axis_index("tok"), lax.axis_index("voc")
    core = band % 2
    quarter = rows // voc_count
    half = rows // 2

    def permute(value, move):
        pairs = []
        for t in range(tok_count):
            for v in range(voc_count):
                to_t, to_v = move(t, v)
                pairs.append((t * voc_count + v, to_t * voc_count + to_v))
        return lax.ppermute(value, AXES, pairs)

    def along_z(value, d):
        return permute(value, lambda t, v: (t ^ (d * side), v))

    def along_y(value, d):
        return permute(value, lambda t, v: (t ^ d, v))

    def across_cores(value):
        return permute(value, lambda t, v: (t, v ^ 1))

    def second_hop(value, d):
        return permute(value, lambda t, v: (t ^ d, v) if v % 2 == 0 else (t, v ^ (2 * d)))

    def third_hop(value, d):
        return permute(value, lambda t, v: (t, v ^ (2 * d)) if v % 2 == 0 else (t ^ d, v))

    spot = jnp.stack([me, band]).astype(jnp.int32)
    block, own_quarter, own_half, table = prepare(
        spot, hidden, norm_gain, targets, lengths, prior_device, prior_row, voc_count
    )
    near = [along_y(own_half, d) for d in range(1, side)]
    arrived = {1: along_z(own_quarter, 1)}
    second = {1: [second_hop(arrived[1], e) for e in range(1, side)]}
    for d in range(2, depth):
        high = 1 << (d.bit_length() - 1)
        arrived[d] = along_z(after(arrived[high], arrived[1], *near) if d > high else own_quarter, d % high or high)
    near_far = [across_cores(n) for n in near]

    head = head_weight
    if width % LANES:
        head = jnp.pad(head_weight, ((0, 0), (0, LANES - width % LANES)))

    pieces, layout = [block], [tuple((("own", 0, 0, i), 0) for i in range(voc_count))]
    for d in range(1, side):
        pieces += [near[d - 1], near_far[d - 1]]
        layout += [tuple((("near", d, e, i), 0) for i in range(voc_count // 2)) for e in range(2)]
    sizes = (rows, width, tok_count, voc_count)
    third, late, late_layout = {}, [], []
    for d in range(1, depth):
        start = arrived[d]
        if d > 1:
            start = after(start, arrived[1], *near)
            second[d] = [second_hop(start, e) for e in range(1, side)]
        gathered = jnp.concatenate([start] + second[d], axis=0)
        if d > 1:
            gathered = after(gathered, *third[1])
        third[d] = [third_hop(gathered, e) for e in range(1, side)]
        pieces += [gathered, across_cores(gathered)]
        layouts = [[tuple(((n, e, 0, i), d * side) for i in range(side)) for n in ("same", "other")] for e in range(side)]
        layout += layouts[0]
        far = list(third[d])
        if d == depth - 1:
            first_stats, first_ends, head = score(pieces, layout, table, head, *sizes, loads=True)
            far = [after(f, first_stats) for f in far]
        for e in range(1, side):
            sent_on = [far[e - 1], across_cores(far[e - 1])]
            if d == 1:
                pieces += sent_on
                layout += layouts[e]
            else:
                late += sent_on
                late_layout += layouts[e]

    (sent,) = score(late, late_layout, table, head, *sizes, earlier=(first_stats, first_ends))
    received = lax.all_to_all(sent, AXES, 0, 0)
    logprob, entropy = finish(spot, lengths, received)
    return logprob.reshape(rows), entropy.reshape(rows)


def solution(mesh):
    in_specs = (P("tok", None), P(), P(None, ("tok", "voc")), P("tok"), P(), P(), P())
    out_specs = (P("tok"), P("tok"))
    return jax.shard_map(body, mesh=mesh, in_specs=in_specs, out_specs=out_specs, check_vma=False)
```

```python
import functools

import jax
import jax.numpy as jnp
from jax import lax
from jax.experimental import pallas as pl
from jax.experimental.pallas import tpu as pltpu
from jax.sharding import PartitionSpec as P

epsilon = 1e-05
LANES = 128
SUB = 16
GROUP = 32
DIGIT = 256
AXES = ("tok", "voc")
VMEM_LIMIT = 24 * 1024 * 1024


def prepare_kernel(spot, *refs):
    sources, (block, quarter, half, table), held, arrivals = refs[:6], refs[6:10], refs[10:16], refs[16]
    fetches = [pltpu.make_async_copy(sources[i], held[i], arrivals.at[i]) for i in range(6)]
    for fetch in fetches:
        fetch.start()
    for fetch in fetches[2:]:
        fetch.wait()
    hidden, gain, targets, lengths, turns, prior_rows = held
    rows, feats = hidden.shape
    me, band = spot[0], spot[1]
    table[0] = me
    table[1] = band
    for u in range(turns.shape[0]):
        table[2 + u] = turns[u]
        table[2 + turns.shape[0] + u] = lengths[u]

    own = targets[...].reshape(1, rows).astype(jnp.float32)
    own = jnp.concatenate([own[:, 1:], own[:, :1]], axis=1)
    high = jnp.floor(own * (1.0 / DIGIT))
    low = own - high * DIGIT
    lane = lax.broadcasted_iota(jnp.int32, (LANES, LANES), 1)
    first_high = jnp.broadcast_to(high[:, rows - 1 :], (LANES, LANES))
    first_low = jnp.broadcast_to(low[:, rows - 1 :], (LANES, LANES))
    for start in range(0, rows, LANES):
        at = slice(start, start + LANES)
        own_high = jnp.broadcast_to(high[:, at], (LANES, LANES)).T
        own_low = jnp.broadcast_to(low[:, at], (LANES, LANES)).T
        digits = jnp.where(
            lane < LANES // 2,
            jnp.where(lane < LANES // 4, own_high, own_low),
            jnp.where(lane < 3 * LANES // 4, first_high, first_low),
        )
        block[at, feats:] = digits.astype(jnp.bfloat16)

    for fetch in fetches[:2]:
        fetch.wait()
    scale = gain[...].reshape(1, feats)

    def norm_rows(step, _):
        at = pl.ds(pl.multiple_of(step * SUB, SUB), SUB)
        value = hidden[at, :].astype(jnp.float32)
        mean = jnp.sum(value * value, axis=1, keepdims=True) * (1.0 / feats)
        block[at, 0:feats] = (value * lax.rsqrt(mean + epsilon) * scale).astype(jnp.bfloat16)
        return 0

    lax.fori_loop(0, rows // SUB, norm_rows, 0, unroll=4)
    asked = jnp.int32(0)
    for u in range(turns.shape[0]):
        asked = jnp.where(turns[u] == me, prior_rows[u], asked)
    end = lengths[me] - 1
    sub = lax.broadcasted_iota(jnp.int32, (SUB, 1), 0)
    values = block[pl.ds(pl.multiple_of(asked // SUB * SUB, SUB), SUB), 0:feats].astype(jnp.float32)
    value = jnp.sum(jnp.where(sub == asked % SUB, values, 0.0), axis=0, keepdims=True)
    at = pl.ds(pl.multiple_of(end // SUB * SUB, SUB), SUB)
    present = block[at, 0:feats].astype(jnp.float32)
    block[at, 0:feats] = jnp.where(sub == end % SUB, value, present).astype(jnp.bfloat16)
    quarter[...] = block[pl.ds(pl.multiple_of(band * quarter.shape[0], SUB), quarter.shape[0]), :]
    half[...] = block[pl.ds(pl.multiple_of(band % 2 * half.shape[0], SUB), half.shape[0]), :]


def prepare(spot, hidden, gain, targets, lengths, turns, prior_rows, voc_count):
    rows, feats = hidden.shape
    sources = (hidden, gain, targets, lengths, turns, prior_rows)
    sources = [pltpu.with_memory_space_constraint(a, pltpu.HBM) for a in sources]
    smem, vmem = pl.BlockSpec(memory_space=pltpu.SMEM), pl.BlockSpec(memory_space=pltpu.VMEM)
    shapes = [jax.ShapeDtypeStruct((n, feats + LANES), hidden.dtype) for n in (rows, rows // voc_count, rows // 2)]
    shapes.append(jax.ShapeDtypeStruct((2 + 2 * turns.shape[0],), jnp.int32))
    held = [pltpu.VMEM(a.shape, a.dtype) for a in sources[:3]] + [pltpu.SMEM(a.shape, a.dtype) for a in sources[3:]]
    return pl.pallas_call(
        prepare_kernel,
        out_shape=shapes,
        in_specs=[smem] + [pl.BlockSpec(memory_space=pltpu.HBM)] * 6,
        out_specs=[vmem] * 3 + [smem],
        scratch_shapes=held + [pltpu.SemaphoreType.DMA((6,))],
        compiler_params=pltpu.CompilerParams(vmem_limit_bytes=VMEM_LIMIT),
    )(spot, *sources)


def load_kernel(stored, head, arrival):
    fetch = pltpu.make_async_copy(stored, head, arrival)
    fetch.start()
    fetch.wait()


def load(head):
    return pl.pallas_call(
        load_kernel,
        out_shape=pltpu.VMEM(head.shape, head.dtype),
        in_specs=[pl.BlockSpec(memory_space=pltpu.HBM)],
        out_specs=pl.BlockSpec(memory_space=pltpu.VMEM),
        scratch_shapes=[pltpu.SemaphoreType.DMA],
        compiler_params=pltpu.CompilerParams(vmem_limit_bytes=VMEM_LIMIT),
        cost_estimate=pl.CostEstimate(flops=0, bytes_accessed=2 * head.size * head.dtype.itemsize, transcendentals=0),
    )(pltpu.with_memory_space_constraint(head, pltpu.HBM))


def place_of(kind, core, band, rows, side, voc_count):
    name, d, e, index = kind
    quarter = rows // voc_count
    if name == "own":
        return index * quarter
    if name == "near":
        return d * rows + (core if e == 0 else 1 - core) * (rows // 2) + index * quarter
    if name == "other":
        core, band = 1 - core, band ^ 1
    y, x = jnp.where(core == 0, index, d), jnp.where(core == 0, d, index)
    return y * rows + (band ^ (2 * x)) * quarter


def score_kernel(layout, rows, width, turn_count, voc_count, collects, table, head, *rest):
    pieces, rest = rest[: len(layout)], rest[len(layout) :]
    if collects:
        earlier, earlier_ends, rest = rest[0], rest[1], rest[2:]
        out, rest = rest[0], rest[1:]
    else:
        out, ends, rest = rest[0], rest[1], rest[2:]
    found = out
    if collects:
        found, rest = rest[0], rest[1:]
    states, even, odd, lines, kept, edges = rest
    feats = head.shape[0]
    tiles = head.shape[1] // LANES
    halves = rows // LANES
    side = voc_count // 2
    size = rows // voc_count
    turns, lengths = 2, 2 + turn_count
    me, band = table[0], table[1]
    core = band % 2
    base = (me * voc_count + band) * width

    offset = jnp.int32(0)
    moved = []
    present = set()
    for ref, parts in zip(pieces, layout):
        for index, (kind, start_block) in enumerate(parts):
            present.update(range(start_block, start_block + side))
            place = jnp.asarray(place_of(kind, core, band, rows, side, voc_count), jnp.int32)
            block = start_block + place // rows
            row = place % rows
            live = jnp.clip(table[lengths + (me ^ block)] - row, 0, size)
            for step in range(0, size, GROUP):

                @pl.when(step < live)
                def _(ref=ref, start=index * size + step, to=offset + step):
                    states[pl.ds(pl.multiple_of(to, GROUP), GROUP), :] = ref[start : start + GROUP, :]

            moved.append((start_block, block, row, offset))
            offset = offset + (live + GROUP - 1) // GROUP * GROUP
    total_rows = offset + GROUP if collects else offset
    count = (total_rows + LANES - 1) // LANES

    sub = lax.broadcasted_iota(jnp.int32, (SUB, 1), 0)
    sub_group = lax.broadcasted_iota(jnp.int32, (GROUP, 1), 0)
    edges[...] = earlier_ends[...].astype(jnp.float32) if collects else jnp.zeros(edges.shape, jnp.float32)
    for line in sorted(present):
        end = table[lengths + (me ^ line)] - 1
        end_row = end // size * size
        at_end, at_first = jnp.int32(-1), jnp.int32(-1)
        for start_block, block, row, to in moved:
            if start_block <= line < start_block + side:
                at_end = jnp.where((block == line) & (row == end_row), to + end % size, at_end)
                at_first = jnp.where((block == line) & (row == 0), to, at_first)

        def row_at(at, columns):
            group = pl.ds(pl.multiple_of(jnp.maximum(at, 0) // SUB * SUB, SUB), SUB)
            values = states[group, columns].astype(jnp.float32)
            return jnp.sum(jnp.where((sub == at % SUB) & (at >= 0), values, 0.0), axis=0, keepdims=True)

        for at, columns in ((at_end, slice(0, feats)), (at_first, slice(feats, feats + LANES))):
            edges[line : line + 1, columns] = edges[line : line + 1, columns] + row_at(at, columns)
    if collects:
        group = pl.ds(pl.multiple_of(offset, GROUP), GROUP)
        states[group, 0:feats] = edges[:, 0:feats].astype(jnp.bfloat16)
        digits = jnp.zeros((GROUP, LANES), jnp.float32)
        for line in range(turn_count):
            asked = me ^ table[turns + (me ^ line)]
            digits = digits + jnp.where(sub_group == asked, edges[line : line + 1, feats:], 0.0)
        states[group, feats:] = pltpu.roll(digits, LANES // 2, 1).astype(jnp.bfloat16)
    else:
        ends[...] = edges[...].astype(jnp.bfloat16)

    lanes = lax.broadcasted_iota(jnp.int32, (SUB, LANES), 1)
    lanes_f = lanes.astype(jnp.float32)
    base_f = base.astype(jnp.float32)

    def multiply(tile, into):
        at = pl.ds(pl.multiple_of(tile * LANES, LANES), LANES)
        into[...] = jnp.dot(states[at, 0:feats], head[...], preferred_element_type=jnp.float32)

    def reduce(tile, logits):
        for row in range(0, LANES, SUB):
            at = slice(row, row + SUB)

            def part(k, at=at):
                value = logits[at, k * LANES : (k + 1) * LANES]
                if (k + 1) * LANES > width:
                    value = jnp.where(lanes < width - k * LANES, value, -1e30)
                return value

            top = part(0)
            for k in range(1, tiles):
                top = jnp.maximum(top, part(k))
            here = pl.ds(pl.multiple_of(tile * LANES + row, SUB), SUB)
            digits = states[here, feats:].astype(jnp.float32)
            digits = jnp.where(lanes < LANES // 4, digits * DIGIT, jnp.where(lanes < LANES // 2, digits, 0.0))
            digits = digits + pltpu.roll(digits, LANES // 2, 1)
            offset = digits + pltpu.roll(digits, LANES // 4, 1) - base_f - lanes_f
            total = jnp.zeros((SUB, LANES), jnp.float32)
            moment = total
            picked = total
            for k in range(tiles):
                value = part(k)
                weight = jnp.exp(value - top)
                total = total + weight
                moment = moment + weight * value
                picked = picked + jnp.where(offset == float(k * LANES), value, 0.0)
            kept[0, at, :] = top
            kept[1, at, :] = total
            kept[2, at, :] = moment
            kept[3, at, :] = picked
        top = kept[0].T
        largest = jnp.max(top, axis=0, keepdims=True)
        factor = jnp.exp(top - largest)
        lines[tile, 0:1, :] = largest
        lines[tile, 1:2, :] = jnp.sum(kept[1].T * factor, axis=0, keepdims=True)
        lines[tile, 2:3, :] = jnp.sum(kept[2].T * factor, axis=0, keepdims=True)
        lines[tile, 3:4, :] = jnp.sum(kept[3].T, axis=0, keepdims=True)

    multiply(0, even)

    def two_tiles(step, _):
        multiply(2 * step + 1, odd)
        reduce(2 * step, even)
        multiply(2 * step + 2, even)
        reduce(2 * step + 1, odd)
        return 0

    lax.fori_loop(0, (count - 1) // 2, two_tiles, 0)

    @pl.when(count % 2 == 0)
    def _():
        multiply(count - 1, odd)
        reduce(count - 2, even)
        reduce(count - 1, odd)

    @pl.when(count % 2 == 1)
    def _():
        reduce(count - 1, even)

    lane = lax.broadcasted_iota(jnp.int32, (8, LANES), 1)
    if collects:
        found[...] = earlier[...]
    for _, block, row, to in moved:
        tile, turned, shift = to // LANES, to % LANES, row % LANES
        back = (LANES - turned) % LANES
        here, following = pltpu.roll(lines[tile], back, 1), pltpu.roll(lines[tile + 1], back, 1)
        value = pltpu.roll(jnp.where(lane < LANES - turned, here, following), shift, 1)
        inside = (lane >= shift) & (lane < shift + size)
        found[block, row // LANES] = jnp.where(inside, value, found[block, row // LANES])

    if collects:
        high = 4 * halves
        line = lax.broadcasted_iota(jnp.int32, (high, LANES), 0)
        lane = lax.broadcasted_iota(jnp.int32, (high, LANES), 1)
        swap = (lane == LANES - 1) & (line >= high - 4)
        edge_lines = jnp.concatenate([lines[offset // LANES, 0:4, :]] * halves, axis=0)
        for turn in range(turn_count):
            at = offset % LANES + (me ^ table[turns + turn])
            prior = pltpu.roll(edge_lines, LANES - 1 - at, 1)
            own = jnp.concatenate([found[me ^ turn, half][0:4, :] for half in range(halves)], axis=0)
            value = jnp.where(swap, prior, own)
            for copy in range(voc_count):
                out[turn * voc_count + copy] = value


def score(pieces, layout, table, head, rows, width, turn_count, voc_count, earlier=()):
    collects = bool(earlier)
    raw_rows = sum(piece.shape[0] for piece in pieces)
    feats, columns = head.shape
    halves = rows // LANES
    smem = pl.BlockSpec(memory_space=pltpu.SMEM)
    vmem = pl.BlockSpec(memory_space=pltpu.VMEM)
    by_block = (turn_count, halves, 8, LANES)
    scratch = []
    if collects:
        result = [jax.ShapeDtypeStruct((turn_count * voc_count, 4 * halves, LANES), jnp.float32)]
    else:
        result = [jax.ShapeDtypeStruct(by_block, jnp.float32)]
        result.append(jax.ShapeDtypeStruct((GROUP, feats + LANES), jnp.bfloat16))
    if collects:
        scratch.append(pltpu.VMEM(by_block, jnp.float32))
    return pl.pallas_call(
        functools.partial(score_kernel, layout, rows, width, turn_count, voc_count, collects),
        out_shape=result,
        in_specs=[smem] + [vmem] * (1 + len(pieces) + len(earlier)),
        out_specs=[vmem] * len(result),
        scratch_shapes=scratch
        + [
            pltpu.VMEM((raw_rows + LANES, feats + LANES), jnp.bfloat16),
            pltpu.VMEM((LANES, columns), jnp.float32),
            pltpu.VMEM((LANES, columns), jnp.float32),
            pltpu.VMEM((raw_rows // LANES + 2, 8, LANES), jnp.float32),
            pltpu.VMEM((4, LANES, LANES), jnp.float32),
            pltpu.VMEM((GROUP, feats + LANES), jnp.float32),
        ],
        compiler_params=pltpu.CompilerParams(vmem_limit_bytes=VMEM_LIMIT),
        cost_estimate=pl.CostEstimate(
            flops=2 * raw_rows * feats * columns,
            bytes_accessed=2 * feats * (raw_rows + columns),
            transcendentals=raw_rows * columns,
        ),
    )(table, head, *pieces, *earlier)


def finish_kernel(spot, lengths, received, logprob, entropy):
    halves = received.shape[1] // 4

    def kind_of(kind):
        return jnp.concatenate([received[:, 4 * h + kind : 4 * h + kind + 1, :] for h in range(halves)], axis=1)

    top = kind_of(0)
    largest = jnp.max(top, axis=0)
    factor = jnp.exp(top - largest[None])
    total = jnp.sum(kind_of(1) * factor, axis=0)
    moment = jnp.sum(kind_of(2) * factor, axis=0)
    picked = jnp.sum(kind_of(3), axis=0)
    normalizer = largest + jnp.log(total)
    half = lax.broadcasted_iota(jnp.int32, largest.shape, 0)
    lane = lax.broadcasted_iota(jnp.int32, largest.shape, 1)
    live = half * LANES + lane < lengths[spot[0]]

    def by_scored_row(value):
        previous = jnp.concatenate([value[halves - 1 :], value[: halves - 1]], axis=0)
        rolled = jnp.concatenate([value[:, LANES - 1 :], value[:, : LANES - 1]], axis=1)
        rolled_previous = jnp.concatenate([previous[:, LANES - 1 :], previous[:, : LANES - 1]], axis=1)
        return jnp.where(live, jnp.where(lane == 0, rolled_previous, rolled), 0.0)

    logprob[...] = by_scored_row(picked - normalizer)
    entropy[...] = by_scored_row(normalizer - moment / total)


def finish(spot, lengths, received):
    smem = pl.BlockSpec(memory_space=pltpu.SMEM)
    vmem = pl.BlockSpec(memory_space=pltpu.VMEM)
    halves = received.shape[1] // 4
    shape = jax.ShapeDtypeStruct((halves, LANES), jnp.float32)
    return pl.pallas_call(
        finish_kernel, out_shape=(shape, shape), in_specs=[smem, smem, vmem], out_specs=(vmem, vmem)
    )(spot, lengths, received)


def after(value, *others):
    return lax.optimization_barrier((value,) + others)[0]


def body(hidden, norm_gain, head_weight, targets, lengths, prior_device, prior_row):
    rows, feats = hidden.shape
    width = head_weight.shape[1]
    tok_count, voc_count = lax.axis_size("tok"), lax.axis_size("voc")
    side = voc_count // 2
    depth = tok_count // side
    me, band = lax.axis_index("tok"), lax.axis_index("voc")
    core = band % 2
    quarter = rows // voc_count
    half = rows // 2

    def permute(value, move):
        pairs = []
        for t in range(tok_count):
            for v in range(voc_count):
                to_t, to_v = move(t, v)
                pairs.append((t * voc_count + v, to_t * voc_count + to_v))
        return lax.ppermute(value, AXES, pairs)

    def along_z(value, d):
        return permute(value, lambda t, v: (t ^ (d * side), v))

    def along_y(value, d):
        return permute(value, lambda t, v: (t ^ d, v))

    def across_cores(value):
        return permute(value, lambda t, v: (t, v ^ 1))

    def second_hop(value, d):
        return permute(value, lambda t, v: (t ^ d, v) if v % 2 == 0 else (t, v ^ (2 * d)))

    def third_hop(value, d):
        return permute(value, lambda t, v: (t, v ^ (2 * d)) if v % 2 == 0 else (t ^ d, v))

    spot = jnp.stack([me, band]).astype(jnp.int32)
    block, own_quarter, own_half, table = prepare(
        spot, hidden, norm_gain, targets, lengths, prior_device, prior_row, voc_count
    )
    near = [along_y(own_half, d) for d in range(1, side)]
    arrived = {1: along_z(own_quarter, 1)}
    head = head_weight
    if width % LANES:
        head = jnp.pad(head_weight, ((0, 0), (0, LANES - width % LANES)))
    head = load(head)
    second = {1: [second_hop(after(arrived[1], head), e) for e in range(1, side)]}
    for d in range(2, depth):
        high = 1 << (d.bit_length() - 1)
        arrived[d] = along_z(after(arrived[high], arrived[1], *near) if d > high else own_quarter, d % high or high)
    near_far = [across_cores(n) for n in near]


    pieces, layout = [block], [tuple((("own", 0, 0, i), 0) for i in range(voc_count))]
    for d in range(1, side):
        pieces += [near[d - 1], near_far[d - 1]]
        layout += [tuple((("near", d, e, i), 0) for i in range(voc_count // 2)) for e in range(2)]
    sizes = (rows, width, tok_count, voc_count)
    third, late, late_layout = {}, [], []
    for d in range(1, depth):
        start = arrived[d]
        if d > 1:
            start = after(start, arrived[1], *near)
            second[d] = [second_hop(start, e) for e in range(1, side)]
        gathered = jnp.concatenate([start] + second[d], axis=0)
        if d > 1:
            gathered = after(gathered, *third[1])
        third[d] = [third_hop(gathered, e) for e in range(1, side)]
        pieces += [gathered, across_cores(gathered)]
        layouts = [[tuple(((n, e, 0, i), d * side) for i in range(side)) for n in ("same", "other")] for e in range(side)]
        layout += layouts[0]
        far = list(third[d])
        if d == depth - 1:
            first_stats, first_ends = score(pieces, layout, table, head, *sizes)
            far = [after(f, first_stats) for f in far]
        for e in range(1, side):
            sent_on = [far[e - 1], across_cores(far[e - 1])]
            if d == 1:
                pieces += sent_on
                layout += layouts[e]
            else:
                late += sent_on
                late_layout += layouts[e]

    (sent,) = score(late, late_layout, table, head, *sizes, earlier=(first_stats, first_ends))
    received = lax.all_to_all(sent, AXES, 0, 0)
    logprob, entropy = finish(spot, lengths, received)
    return logprob.reshape(rows), entropy.reshape(rows)


def solution(mesh):
    in_specs = (P("tok", None), P(), P(None, ("tok", "voc")), P("tok"), P(), P(), P())
    out_specs = (P("tok"), P("tok"))
    return jax.shard_map(body, mesh=mesh, in_specs=in_specs, out_specs=out_specs, check_vma=False)
```

```python
import functools

import jax
import jax.numpy as jnp
from jax import lax
from jax.experimental import pallas as pl
from jax.experimental.pallas import tpu as pltpu
from jax.sharding import PartitionSpec as P

epsilon = 1e-05
LANES = 128
SUB = 16
GROUP = 32
DIGIT = 256
AXES = ("tok", "voc")
VMEM_LIMIT = 24 * 1024 * 1024


def prepare_kernel(spot, *refs):
    sources, (block, quarter, half, table), held, arrivals = refs[:6], refs[6:10], refs[10:16], refs[16]
    fetches = [pltpu.make_async_copy(sources[i], held[i], arrivals.at[i]) for i in range(6)]
    for fetch in fetches:
        fetch.start()
    for fetch in fetches[2:]:
        fetch.wait()
    hidden, gain, targets, lengths, turns, prior_rows = held
    rows, feats = hidden.shape
    me, band = spot[0], spot[1]
    table[0] = me
    table[1] = band
    for u in range(turns.shape[0]):
        table[2 + u] = turns[u]
        table[2 + turns.shape[0] + u] = lengths[u]

    own = targets[...].reshape(1, rows).astype(jnp.float32)
    own = jnp.concatenate([own[:, 1:], own[:, :1]], axis=1)
    high = jnp.floor(own * (1.0 / DIGIT))
    low = own - high * DIGIT
    lane = lax.broadcasted_iota(jnp.int32, (LANES, LANES), 1)
    first_high = jnp.broadcast_to(high[:, rows - 1 :], (LANES, LANES))
    first_low = jnp.broadcast_to(low[:, rows - 1 :], (LANES, LANES))
    for start in range(0, rows, LANES):
        at = slice(start, start + LANES)
        own_high = jnp.broadcast_to(high[:, at], (LANES, LANES)).T
        own_low = jnp.broadcast_to(low[:, at], (LANES, LANES)).T
        digits = jnp.where(
            lane < LANES // 2,
            jnp.where(lane < LANES // 4, own_high, own_low),
            jnp.where(lane < 3 * LANES // 4, first_high, first_low),
        )
        block[at, feats:] = digits.astype(jnp.bfloat16)

    for fetch in fetches[:2]:
        fetch.wait()
    scale = gain[...].reshape(1, feats)

    def norm_rows(step, _):
        at = pl.ds(pl.multiple_of(step * SUB, SUB), SUB)
        value = hidden[at, :].astype(jnp.float32)
        mean = jnp.sum(value * value, axis=1, keepdims=True) * (1.0 / feats)
        block[at, 0:feats] = (value * lax.rsqrt(mean + epsilon) * scale).astype(jnp.bfloat16)
        return 0

    lax.fori_loop(0, rows // SUB, norm_rows, 0, unroll=4)
    asked = jnp.int32(0)
    for u in range(turns.shape[0]):
        asked = jnp.where(turns[u] == me, prior_rows[u], asked)
    end = lengths[me] - 1
    sub = lax.broadcasted_iota(jnp.int32, (SUB, 1), 0)
    values = block[pl.ds(pl.multiple_of(asked // SUB * SUB, SUB), SUB), 0:feats].astype(jnp.float32)
    value = jnp.sum(jnp.where(sub == asked % SUB, values, 0.0), axis=0, keepdims=True)
    at = pl.ds(pl.multiple_of(end // SUB * SUB, SUB), SUB)
    present = block[at, 0:feats].astype(jnp.float32)
    block[at, 0:feats] = jnp.where(sub == end % SUB, value, present).astype(jnp.bfloat16)
    quarter[...] = block[pl.ds(pl.multiple_of(band * quarter.shape[0], SUB), quarter.shape[0]), :]
    half[...] = block[pl.ds(pl.multiple_of(band % 2 * half.shape[0], SUB), half.shape[0]), :]


def prepare(spot, hidden, gain, targets, lengths, turns, prior_rows, voc_count):
    rows, feats = hidden.shape
    sources = (hidden, gain, targets, lengths, turns, prior_rows)
    sources = [pltpu.with_memory_space_constraint(a, pltpu.HBM) for a in sources]
    smem, vmem = pl.BlockSpec(memory_space=pltpu.SMEM), pl.BlockSpec(memory_space=pltpu.VMEM)
    shapes = [jax.ShapeDtypeStruct((n, feats + LANES), hidden.dtype) for n in (rows, rows // voc_count, rows // 2)]
    shapes.append(jax.ShapeDtypeStruct((2 + 2 * turns.shape[0],), jnp.int32))
    held = [pltpu.VMEM(a.shape, a.dtype) for a in sources[:3]] + [pltpu.SMEM(a.shape, a.dtype) for a in sources[3:]]
    return pl.pallas_call(
        prepare_kernel,
        out_shape=shapes,
        in_specs=[smem] + [pl.BlockSpec(memory_space=pltpu.HBM)] * 6,
        out_specs=[vmem] * 3 + [smem],
        scratch_shapes=held + [pltpu.SemaphoreType.DMA((6,))],
        compiler_params=pltpu.CompilerParams(vmem_limit_bytes=VMEM_LIMIT),
    )(spot, *sources)


def load_kernel(stored, head, arrival):
    fetch = pltpu.make_async_copy(stored, head, arrival)
    fetch.start()
    fetch.wait()


def load(head):
    return pl.pallas_call(
        load_kernel,
        out_shape=pltpu.VMEM(head.shape, head.dtype),
        in_specs=[pl.BlockSpec(memory_space=pltpu.HBM)],
        out_specs=pl.BlockSpec(memory_space=pltpu.VMEM),
        scratch_shapes=[pltpu.SemaphoreType.DMA],
        compiler_params=pltpu.CompilerParams(vmem_limit_bytes=VMEM_LIMIT),
        cost_estimate=pl.CostEstimate(flops=0, bytes_accessed=2 * head.size * head.dtype.itemsize, transcendentals=0),
    )(pltpu.with_memory_space_constraint(head, pltpu.HBM))


def place_of(kind, core, band, rows, side, voc_count):
    name, d, e, index = kind
    quarter = rows // voc_count
    if name == "own":
        return index * quarter
    if name == "near":
        return d * rows + (core if e == 0 else 1 - core) * (rows // 2) + index * quarter
    if name == "other":
        core, band = 1 - core, band ^ 1
    y, x = jnp.where(core == 0, index, d), jnp.where(core == 0, d, index)
    return y * rows + (band ^ (2 * x)) * quarter


def score_kernel(layout, rows, width, turn_count, voc_count, collects, table, head, *rest):
    pieces, rest = rest[: len(layout)], rest[len(layout) :]
    if collects:
        earlier, earlier_ends, rest = rest[0], rest[1], rest[2:]
        out, rest = rest[0], rest[1:]
    else:
        out, ends, rest = rest[0], rest[1], rest[2:]
    found = out
    if collects:
        found, rest = rest[0], rest[1:]
    states, even, odd, lines, kept, edges = rest
    feats = head.shape[0]
    tiles = head.shape[1] // LANES
    halves = rows // LANES
    side = voc_count // 2
    size = rows // voc_count
    turns, lengths = 2, 2 + turn_count
    me, band = table[0], table[1]
    core = band % 2
    base = (me * voc_count + band) * width

    offset = jnp.int32(0)
    moved = []
    present = set()
    for ref, parts in zip(pieces, layout):
        for index, (kind, start_block) in enumerate(parts):
            present.update(range(start_block, start_block + side))
            place = jnp.asarray(place_of(kind, core, band, rows, side, voc_count), jnp.int32)
            block = start_block + place // rows
            row = place % rows
            live = jnp.clip(table[lengths + (me ^ block)] - row, 0, size)
            for step in range(0, size, GROUP):

                @pl.when(step < live)
                def _(ref=ref, start=index * size + step, to=offset + step):
                    states[pl.ds(pl.multiple_of(to, GROUP), GROUP), :] = ref[start : start + GROUP, :]

            moved.append((start_block, block, row, offset))
            offset = offset + (live + GROUP - 1) // GROUP * GROUP
    total_rows = offset + GROUP if collects else offset
    count = (total_rows + LANES - 1) // LANES

    sub = lax.broadcasted_iota(jnp.int32, (SUB, 1), 0)
    sub_group = lax.broadcasted_iota(jnp.int32, (GROUP, 1), 0)
    edges[...] = earlier_ends[...].astype(jnp.float32) if collects else jnp.zeros(edges.shape, jnp.float32)
    for line in sorted(present):
        end = table[lengths + (me ^ line)] - 1
        end_row = end // size * size
        at_end, at_first = jnp.int32(-1), jnp.int32(-1)
        for start_block, block, row, to in moved:
            if start_block <= line < start_block + side:
                at_end = jnp.where((block == line) & (row == end_row), to + end % size, at_end)
                at_first = jnp.where((block == line) & (row == 0), to, at_first)

        def row_at(at, columns):
            group = pl.ds(pl.multiple_of(jnp.maximum(at, 0) // SUB * SUB, SUB), SUB)
            values = states[group, columns].astype(jnp.float32)
            return jnp.sum(jnp.where((sub == at % SUB) & (at >= 0), values, 0.0), axis=0, keepdims=True)

        for at, columns in ((at_end, slice(0, feats)), (at_first, slice(feats, feats + LANES))):
            edges[line : line + 1, columns] = edges[line : line + 1, columns] + row_at(at, columns)
    if collects:
        group = pl.ds(pl.multiple_of(offset, GROUP), GROUP)
        states[group, 0:feats] = edges[:, 0:feats].astype(jnp.bfloat16)
        digits = jnp.zeros((GROUP, LANES), jnp.float32)
        for line in range(turn_count):
            asked = me ^ table[turns + (me ^ line)]
            digits = digits + jnp.where(sub_group == asked, edges[line : line + 1, feats:], 0.0)
        states[group, feats:] = pltpu.roll(digits, LANES // 2, 1).astype(jnp.bfloat16)
    else:
        ends[...] = edges[...].astype(jnp.bfloat16)

    lanes = lax.broadcasted_iota(jnp.int32, (SUB, LANES), 1)
    lanes_f = lanes.astype(jnp.float32)
    base_f = base.astype(jnp.float32)

    def multiply(tile, into):
        at = pl.ds(pl.multiple_of(tile * LANES, LANES), LANES)
        into[...] = jnp.dot(states[at, 0:feats], head[...], preferred_element_type=jnp.float32)

    def reduce(tile, logits):
        for row in range(0, LANES, SUB):
            at = slice(row, row + SUB)

            def part(k, at=at):
                value = logits[at, k * LANES : (k + 1) * LANES]
                if (k + 1) * LANES > width:
                    value = jnp.where(lanes < width - k * LANES, value, -1e30)
                return value

            top = part(0)
            for k in range(1, tiles):
                top = jnp.maximum(top, part(k))
            here = pl.ds(pl.multiple_of(tile * LANES + row, SUB), SUB)
            digits = states[here, feats:].astype(jnp.float32)
            digits = jnp.where(lanes < LANES // 4, digits * DIGIT, jnp.where(lanes < LANES // 2, digits, 0.0))
            digits = digits + pltpu.roll(digits, LANES // 2, 1)
            offset = digits + pltpu.roll(digits, LANES // 4, 1) - base_f - lanes_f
            total = jnp.zeros((SUB, LANES), jnp.float32)
            moment = total
            picked = total
            for k in range(tiles):
                value = part(k)
                weight = jnp.exp(value - top)
                total = total + weight
                moment = moment + weight * value
                picked = picked + jnp.where(offset == float(k * LANES), value, 0.0)
            kept[0, at, :] = top
            kept[1, at, :] = total
            kept[2, at, :] = moment
            kept[3, at, :] = picked
        top = kept[0].T
        largest = jnp.max(top, axis=0, keepdims=True)
        factor = jnp.exp(top - largest)
        lines[tile, 0:1, :] = largest
        lines[tile, 1:2, :] = jnp.sum(kept[1].T * factor, axis=0, keepdims=True)
        lines[tile, 2:3, :] = jnp.sum(kept[2].T * factor, axis=0, keepdims=True)
        lines[tile, 3:4, :] = jnp.sum(kept[3].T, axis=0, keepdims=True)

    multiply(0, even)

    def two_tiles(step, _):
        multiply(2 * step + 1, odd)
        reduce(2 * step, even)
        multiply(2 * step + 2, even)
        reduce(2 * step + 1, odd)
        return 0

    lax.fori_loop(0, (count - 1) // 2, two_tiles, 0)

    @pl.when(count % 2 == 0)
    def _():
        multiply(count - 1, odd)
        reduce(count - 2, even)
        reduce(count - 1, odd)

    @pl.when(count % 2 == 1)
    def _():
        reduce(count - 1, even)

    lane = lax.broadcasted_iota(jnp.int32, (8, LANES), 1)
    if collects:
        found[...] = earlier[...]
    for _, block, row, to in moved:
        tile, turned, shift = to // LANES, to % LANES, row % LANES
        back = (LANES - turned) % LANES
        here, following = pltpu.roll(lines[tile], back, 1), pltpu.roll(lines[tile + 1], back, 1)
        value = pltpu.roll(jnp.where(lane < LANES - turned, here, following), shift, 1)
        inside = (lane >= shift) & (lane < shift + size)
        found[block, row // LANES] = jnp.where(inside, value, found[block, row // LANES])

    if collects:
        high = 4 * halves
        line = lax.broadcasted_iota(jnp.int32, (high, LANES), 0)
        lane = lax.broadcasted_iota(jnp.int32, (high, LANES), 1)
        swap = (lane == LANES - 1) & (line >= high - 4)
        edge_lines = jnp.concatenate([lines[offset // LANES, 0:4, :]] * halves, axis=0)
        for turn in range(turn_count):
            at = offset % LANES + (me ^ table[turns + turn])
            prior = pltpu.roll(edge_lines, LANES - 1 - at, 1)
            own = jnp.concatenate([found[me ^ turn, half][0:4, :] for half in range(halves)], axis=0)
            value = jnp.where(swap, prior, own)
            for copy in range(voc_count):
                out[turn * voc_count + copy] = value


def score(pieces, layout, table, head, rows, width, turn_count, voc_count, earlier=()):
    collects = bool(earlier)
    raw_rows = sum(piece.shape[0] for piece in pieces)
    feats, columns = head.shape
    halves = rows // LANES
    smem = pl.BlockSpec(memory_space=pltpu.SMEM)
    vmem = pl.BlockSpec(memory_space=pltpu.VMEM)
    by_block = (turn_count, halves, 8, LANES)
    scratch = []
    if collects:
        result = [jax.ShapeDtypeStruct((turn_count * voc_count, 4 * halves, LANES), jnp.float32)]
    else:
        result = [jax.ShapeDtypeStruct(by_block, jnp.float32)]
        result.append(jax.ShapeDtypeStruct((GROUP, feats + LANES), jnp.bfloat16))
    if collects:
        scratch.append(pltpu.VMEM(by_block, jnp.float32))
    return pl.pallas_call(
        functools.partial(score_kernel, layout, rows, width, turn_count, voc_count, collects),
        out_shape=result,
        in_specs=[smem] + [vmem] * (1 + len(pieces) + len(earlier)),
        out_specs=[vmem] * len(result),
        scratch_shapes=scratch
        + [
            pltpu.VMEM((raw_rows + LANES, feats + LANES), jnp.bfloat16),
            pltpu.VMEM((LANES, columns), jnp.float32),
            pltpu.VMEM((LANES, columns), jnp.float32),
            pltpu.VMEM((raw_rows // LANES + 2, 8, LANES), jnp.float32),
            pltpu.VMEM((4, LANES, LANES), jnp.float32),
            pltpu.VMEM((GROUP, feats + LANES), jnp.float32),
        ],
        compiler_params=pltpu.CompilerParams(vmem_limit_bytes=VMEM_LIMIT),
        cost_estimate=pl.CostEstimate(
            flops=2 * raw_rows * feats * columns,
            bytes_accessed=2 * feats * (raw_rows + columns),
            transcendentals=raw_rows * columns,
        ),
    )(table, head, *pieces, *earlier)


def finish_kernel(spot, lengths, received, logprob, entropy):
    halves = received.shape[1] // 4

    def kind_of(kind):
        return jnp.concatenate([received[:, 4 * h + kind : 4 * h + kind + 1, :] for h in range(halves)], axis=1)

    top = kind_of(0)
    largest = jnp.max(top, axis=0)
    factor = jnp.exp(top - largest[None])
    total = jnp.sum(kind_of(1) * factor, axis=0)
    moment = jnp.sum(kind_of(2) * factor, axis=0)
    picked = jnp.sum(kind_of(3), axis=0)
    normalizer = largest + jnp.log(total)
    half = lax.broadcasted_iota(jnp.int32, largest.shape, 0)
    lane = lax.broadcasted_iota(jnp.int32, largest.shape, 1)
    live = half * LANES + lane < lengths[spot[0]]

    def by_scored_row(value):
        previous = jnp.concatenate([value[halves - 1 :], value[: halves - 1]], axis=0)
        rolled = jnp.concatenate([value[:, LANES - 1 :], value[:, : LANES - 1]], axis=1)
        rolled_previous = jnp.concatenate([previous[:, LANES - 1 :], previous[:, : LANES - 1]], axis=1)
        return jnp.where(live, jnp.where(lane == 0, rolled_previous, rolled), 0.0)

    logprob[...] = by_scored_row(picked - normalizer)
    entropy[...] = by_scored_row(normalizer - moment / total)


def finish(spot, lengths, received):
    smem = pl.BlockSpec(memory_space=pltpu.SMEM)
    vmem = pl.BlockSpec(memory_space=pltpu.VMEM)
    halves = received.shape[1] // 4
    shape = jax.ShapeDtypeStruct((halves, LANES), jnp.float32)
    return pl.pallas_call(
        finish_kernel, out_shape=(shape, shape), in_specs=[smem, smem, vmem], out_specs=(vmem, vmem)
    )(spot, lengths, received)


def after(value, *others):
    return lax.optimization_barrier((value,) + others)[0]


def body(hidden, norm_gain, head_weight, targets, lengths, prior_device, prior_row):
    rows, feats = hidden.shape
    width = head_weight.shape[1]
    tok_count, voc_count = lax.axis_size("tok"), lax.axis_size("voc")
    side = voc_count // 2
    depth = tok_count // side
    me, band = lax.axis_index("tok"), lax.axis_index("voc")
    core = band % 2
    quarter = rows // voc_count
    half = rows // 2

    def permute(value, move):
        pairs = []
        for t in range(tok_count):
            for v in range(voc_count):
                to_t, to_v = move(t, v)
                pairs.append((t * voc_count + v, to_t * voc_count + to_v))
        return lax.ppermute(value, AXES, pairs)

    def along_z(value, d):
        return permute(value, lambda t, v: (t ^ (d * side), v))

    def along_y(value, d):
        return permute(value, lambda t, v: (t ^ d, v))

    def across_cores(value):
        return permute(value, lambda t, v: (t, v ^ 1))

    def second_hop(value, d):
        return permute(value, lambda t, v: (t ^ d, v) if v % 2 == 0 else (t, v ^ (2 * d)))

    def third_hop(value, d):
        return permute(value, lambda t, v: (t, v ^ (2 * d)) if v % 2 == 0 else (t ^ d, v))

    spot = jnp.stack([me, band]).astype(jnp.int32)
    block, own_quarter, own_half, table = prepare(
        spot, hidden, norm_gain, targets, lengths, prior_device, prior_row, voc_count
    )
    near = [along_y(own_half, d) for d in range(1, side)]
    arrived = {1: along_z(own_quarter, 1)}
    head = head_weight
    if width % LANES:
        head = jnp.pad(head_weight, ((0, 0), (0, LANES - width % LANES)))
    head = load(head)
    second = {1: [second_hop(after(arrived[1], head), e) for e in range(1, side)]}
    for d in range(2, depth):
        high = 1 << (d.bit_length() - 1)
        arrived[d] = along_z(after(arrived[high], arrived[1], *near) if d > high else own_quarter, d % high or high)
    near_far = [across_cores(n) for n in near]


    pieces, layout = [block], [tuple((("own", 0, 0, i), 0) for i in range(voc_count))]
    for d in range(1, side):
        pieces += [near[d - 1], near_far[d - 1]]
        layout += [tuple((("near", d, e, i), 0) for i in range(voc_count // 2)) for e in range(2)]
    sizes = (rows, width, tok_count, voc_count)
    third, late, late_layout = {}, [], []
    for d in range(1, depth):
        start = arrived[d]
        if d > 1:
            start = after(start, arrived[1], *near)
            second[d] = [second_hop(start, e) for e in range(1, side)]
        gathered = jnp.concatenate([start] + second[d], axis=0)
        if d == 2:
            gathered = after(gathered, *third[1])
        third[d] = [third_hop(gathered, e) for e in range(1, side)]
        pieces += [gathered, across_cores(gathered)]
        layouts = [[tuple(((n, e, 0, i), d * side) for i in range(side)) for n in ("same", "other")] for e in range(side)]
        layout += layouts[0]
        far = list(third[d])
        if d == depth - 1:
            first_stats, first_ends = score(pieces, layout, table, head, *sizes)
            far = [after(f, first_stats) for f in far]
        for e in range(1, side):
            sent_on = [far[e - 1], across_cores(far[e - 1])]
            if d == 1:
                pieces += sent_on
                layout += layouts[e]
            else:
                late += sent_on
                late_layout += layouts[e]

    (sent,) = score(late, late_layout, table, head, *sizes, earlier=(first_stats, first_ends))
    received = lax.all_to_all(sent, AXES, 0, 0)
    logprob, entropy = finish(spot, lengths, received)
    return logprob.reshape(rows), entropy.reshape(rows)


def solution(mesh):
    in_specs = (P("tok", None), P(), P(None, ("tok", "voc")), P("tok"), P(), P(), P())
    out_specs = (P("tok"), P("tok"))
    return jax.shard_map(body, mesh=mesh, in_specs=in_specs, out_specs=out_specs, check_vma=False)
```
